32 devices in a mesh: fsdp: 4 (over x, core), tp: 8 (over z, y).
Axes of the slice: x: 2, y: 2, z: 4, core: 2. Of those that a mesh axis runs over, the one named last changes fastest.
Arguments:
- activations: bfloat16 [16384, 1280], P(('fsdp', 'tp')), may hold values from -6 to 6
- cotangent: bfloat16 [16384, 1280], P(('fsdp', 'tp'))
- lengths: int32 [8, 20], P('fsdp'), may hold values from 0 to 1024, as said below
- positions: int32 [2, 16384], P(None, 'fsdp'), may hold values from 0 to 127, as said below
- weights: float32 [1280, 12, 1280], P('fsdp', None, 'tp')
- first_moment: float32 [1280, 12, 1280], P('fsdp', None, 'tp')
- second_moment: float32 [1280, 12, 1280], P('fsdp', None, 'tp')
- vectors: float32 [13, 1280], replicated
- vector_first: float32 [13, 1280], replicated
- vector_second: float32 [13, 1280], replicated
Outputs:
- block_output: bfloat16 [16384, 1280], P(('fsdp', 'tp'))
- input_grad: bfloat16 [16384, 1280], P(('fsdp', 'tp'))
- next_first: float32 [1280, 12, 1280], P('fsdp', None, 'tp')
- next_second: float32 [1280, 12, 1280], P('fsdp', None, 'tp')
- next_weights: float32 [1280, 12, 1280], P('fsdp', None, 'tp')
- next_vector_first: float32 [13, 1280], replicated
- next_vector_second: float32 [13, 1280], replicated
- next_vectors: float32 [13, 1280], replicated
The draws below stay inside these ranges and needn't reach their ends.
Inputs may be any that keep to these rules, and one draw needn't show every extreme that they name: `lengths`: each row lists its pictures' patch counts, each from 100 to 1024, then zeros; a row's counts sum to at most 2048; one of each row's first two pictures has exactly 1024 patches. `positions`: A picture's patches are numbered row by row with a width of 8 to 16 patches; padding patches have 0 and 0.
All inputs are finite; a program needn't handle non-finite values.
Results may differ from the reference program's by a relative error of at most 0.025.
Values may be sent and summed in bfloat16 or wider, within the bound.
No kernel may reach another device: no remote copies, remote signals or barrier semaphores. Data moves between devices by JAX's collectives and lax.ppermute only.
A program may use at most 192 MiB of HBM per device.

```python
import math
import jax
import jax.numpy as jnp
import numpy as np
from jax import lax

D = 1280
H = 16
HD = 80
SEQ = 2048
ROWS = 2
PICS = 20
PIC_MIN = 100
PIC_MAX = 1024
STEP = 10
NROWS = 8
TOKENS = 16384


slot_spread = np.array([1.0, 1.0, 1.0, 8.0, 1.0, 1.0, 1.0, 1.0, 0.5, 0.5, 0.5, 0.5], dtype=np.float32)


slot_grad = np.array([1.5, 1.5, 1.5, 0.2, 0.25, 0.25, 0.25, 0.25, 0.6, 0.6, 0.6, 0.6], dtype=np.float32)


row_grad = np.array([2.5, 2.5, 0.5, 0.5, 1.4, 1.0, 1.5, 1.5, 1.5, 0.25, 0.25, 0.25, 0.25], dtype=np.float32)


def picture_layout(key):
    key_len, key_pick, key_wide = jax.random.split(key, 3)
    raw = jax.random.randint(key_len, (NROWS, PICS), PIC_MIN, PIC_MAX + 1)
    pick = jax.random.randint(key_pick, (NROWS, 1), 0, 2)
    slot = jnp.arange(PICS, dtype=jnp.int32)[None, :]
    raw = jnp.where(slot == pick, PIC_MAX, raw)
    ends = jnp.cumsum(raw, axis=1)
    lengths = jnp.where(ends <= SEQ, raw, 0)
    widths = jax.random.randint(key_wide, (NROWS, PICS), 8, 17)
    widths = jnp.where(slot == pick, 8, widths)
    return (lengths.astype(jnp.int32), widths.astype(jnp.int32))


def draw_lengths(key, part):
    lengths, widths = picture_layout(key)
    return lengths


def draw_positions(key, part):
    lengths, widths = picture_layout(key)
    ends = jnp.cumsum(lengths, axis=1).astype(jnp.int32)
    starts = ends - lengths
    spots = jnp.arange(SEQ, dtype=jnp.int32)
    picture = jnp.sum((spots[None, :, None] >= ends[:, None, :]).astype(jnp.int32), axis=2)
    valid = picture < PICS
    index = jnp.minimum(picture, PICS - 1)
    begin = jnp.take_along_axis(starts, index, axis=1)
    across = jnp.take_along_axis(widths, index, axis=1)
    offset = spots[None, :] - begin
    upward = jnp.where(valid, offset // across, 0)
    sideways = jnp.where(valid, offset % across, 0)
    return jnp.stack([upward.reshape(-1), sideways.reshape(-1)]).astype(jnp.int32)


def draw_cotangent(key, part):
    key = jax.random.fold_in(key, 5)
    place = jnp.arange(TOKENS, dtype=jnp.int32)
    span = ROWS * SEQ
    outer = (place // span).astype(jnp.float32) * (span / TOKENS)
    inner = (place % span).astype(jnp.float32) / span
    noise = jax.random.normal(key, (TOKENS, D), jnp.float32)
    factor = 0.25 * (1.0 + 2.0 * outer) * (1.0 + 2.0 * inner)
    return (factor[:, None] * noise).astype(jnp.bfloat16)


def draw_weights(key, part):
    key = jax.random.fold_in(key, 11)
    scale = jnp.asarray(slot_spread)[None, :, None] / math.sqrt(D)
    noise = jax.random.normal(key, (D, 12, D), jnp.float32)
    return noise * scale


def draw_first_moment(key, part):
    key = jax.random.fold_in(key, 21)
    size = jnp.asarray(slot_grad)[None, :, None] * math.sqrt(TOKENS)
    return 0.11 * size * jax.random.normal(key, (D, 12, D), jnp.float32)


def draw_second_moment(key, part):
    key = jax.random.fold_in(key, 22)
    size = jnp.asarray(slot_grad)[None, :, None] * math.sqrt(TOKENS)
    factor = jnp.exp(jax.random.uniform(key, (D, 12, D), jnp.float32, 0.0, math.log(4.0)))
    return 0.001 * size * size * factor


def draw_vectors(key, part):
    key = jax.random.fold_in(key, 31)
    noise = jax.random.normal(key, (13, D), jnp.float32)
    rows = jnp.arange(13, dtype=jnp.int32)[:, None]
    is_gain = (rows == 0) | (rows == 2)
    return jnp.where(is_gain, 1.0 + 0.2 * noise, 0.1 * noise)


def draw_vector_first(key, part):
    key = jax.random.fold_in(key, 41)
    size = jnp.asarray(row_grad)[:, None] * math.sqrt(TOKENS)
    return 0.11 * size * jax.random.normal(key, (13, D), jnp.float32)


def draw_vector_second(key, part):
    key = jax.random.fold_in(key, 42)
    size = jnp.asarray(row_grad)[:, None] * math.sqrt(TOKENS)
    factor = jnp.exp(jax.random.uniform(key, (13, D), jnp.float32, 0.0, math.log(4.0)))
    return 0.001 * size * size * factor


def steps_of(rng, dims, cuts, low, largest):
    def one(dim, blocks):
        draws = jax.random.uniform(jax.random.fold_in(jax.random.fold_in(rng, 6), dim), (blocks,), jnp.float32, low / len(cuts), largest / len(cuts))
        return jnp.repeat(jnp.exp(draws), dims[dim] // blocks).reshape((-1,) + (1,) * (len(dims) - dim - 1))

    loudness = one(*cuts[0])
    for cut in cuts[1:]:
        loudness = loudness * one(*cut)
    return loudness


def scatter_about(rng, shape, width, bound, cuts=(), held_as=jnp.bfloat16):
    values = width * jax.random.normal(rng, shape, jnp.float32)
    if cuts:
        values = values * steps_of(rng, shape, cuts, -0.22, 0.18)
    return jnp.clip(values, -bound, bound).astype(held_as)


def setup_inputs(seed: int = 0) -> dict:
    arg_keys = jax.random.split(jax.random.key(seed), 11)
    activations = scatter_about(arg_keys[0], (TOKENS, D), 1.0, 6.0, ((0, 32),))
    cotangent = draw_cotangent(jax.random.fold_in(arg_keys[10], 71), 0)
    lengths = draw_lengths(jax.random.fold_in(arg_keys[10], 71), 0)
    positions = draw_positions(jax.random.fold_in(arg_keys[10], 71), 0)
    weights = draw_weights(jax.random.fold_in(arg_keys[10], 71), 0)
    first_moment = draw_first_moment(jax.random.fold_in(arg_keys[10], 71), 0)
    second_moment = draw_second_moment(jax.random.fold_in(arg_keys[10], 71), 0)
    vectors = draw_vectors(jax.random.fold_in(arg_keys[10], 71), 0)
    vector_first = draw_vector_first(jax.random.fold_in(arg_keys[10], 71), 0)
    vector_second = draw_vector_second(jax.random.fold_in(arg_keys[10], 71), 0)
    return dict(activations=activations, cotangent=cotangent, lengths=lengths, positions=positions, weights=weights, first_moment=first_moment, second_moment=second_moment, vectors=vectors, vector_first=vector_first, vector_second=vector_second)


@jax.custom_vjp
def low(v):
    return lax.optimization_barrier(v.astype(jnp.bfloat16)).astype(jnp.float32)

@jax.custom_vjp
def low_back(v):
    return v

def low_keep(v):
    return (low(v), None)

def low_pass(kept, grad):
    return (grad,)

def back_keep(v):
    return (v, None)

def back_low(kept, grad):
    return (low(grad),)
low.defvjp(low_keep, low_pass)
low_back.defvjp(back_keep, back_low)
norm_eps = 1e-06
beta_first = 0.9
beta_second = 0.999
adam_eps = 1e-08
rate_matrix = 0.08
rate_vector = 0.6
decay_matrix = 0.05
gelu_slope = 1.702
masked_score = -1e+30

def picture_ids(lengths):
    ends = jnp.cumsum(lengths, axis=1).astype(jnp.int32)
    spots = jnp.arange(SEQ, dtype=jnp.int32)
    return lax.optimization_barrier(jnp.sum((spots[None, :, None] >= ends[:, None, :]).astype(jnp.int32), axis=2))

def rotary_tables(positions):
    quarter = HD // 4
    freq = 10000.0 ** (-jnp.arange(quarter, dtype=jnp.float32) * 4.0 / HD)
    upward = positions[0].astype(jnp.float32)[:, None] * freq[None, :]
    sideways = positions[1].astype(jnp.float32)[:, None] * freq[None, :]
    angle = jnp.concatenate([upward, sideways], axis=1)
    return (jnp.cos(angle), jnp.sin(angle))

def rotate(value, cosine, sine):
    half = HD // 2
    first = value[..., :half]
    second = value[..., half:]
    cos_part = cosine[:, None, :]
    sin_part = sine[:, None, :]
    return jnp.concatenate([first * cos_part - second * sin_part, second * cos_part + first * sin_part], axis=-1)

def layer_norm(value, gain, shift):
    center = value - lax.optimization_barrier(jnp.mean(value, axis=-1, keepdims=True))
    spread = lax.optimization_barrier(jnp.mean(center * center, axis=-1, keepdims=True))
    return center * lax.rsqrt(spread + norm_eps) * gain + shift

def quick_gelu(value):
    return value * jax.nn.sigmoid(gelu_slope * value)

def adam_update(param, grad, first, second, rate, decay):
    first = beta_first * first + (1.0 - beta_first) * grad
    second = beta_second * second + (1.0 - beta_second) * grad * grad
    first_hat = first / (1.0 - beta_first ** STEP)
    second_hat = second / (1.0 - beta_second ** STEP)
    fresh = param - rate * (first_hat / (jnp.sqrt(second_hat) + adam_eps) + decay * param)
    return (first, second, fresh)

def row_attention(pieces):
    query, keys, values, ids = pieces
    highest = lax.Precision.HIGHEST
    scores = jnp.einsum('qhc,khc->hqk', query, keys, precision=highest) * HD ** (-0.5)
    scores = low_back(scores)
    scores = jnp.where((ids[:, None] == ids[None, :])[None], scores, masked_score)
    top = lax.optimization_barrier(jnp.max(scores, axis=2, keepdims=True))
    expo = jnp.exp(scores - top)
    probs = low(expo / lax.optimization_barrier(jnp.sum(expo, axis=2, keepdims=True)))
    return jnp.einsum('hqk,khc->qhc', probs, values, precision=highest)

def forward(inputs, weights, vectors, ids, cosine, sine):
    highest = lax.Precision.HIGHEST
    count = inputs.shape[0]
    rows = count // SEQ
    early_norm = low(layer_norm(inputs, vectors[0], vectors[1]))
    heads_pre = jnp.einsum('td,dsc->tsc', early_norm, weights[:, 0:3, :], precision=highest) + vectors[6:9][None, :, :]
    heads_pre = low_back(heads_pre)
    query = low(rotate(heads_pre[:, 0, :].reshape(count, H, HD), cosine, sine))
    keys = low(rotate(heads_pre[:, 1, :].reshape(count, H, HD), cosine, sine))
    values = low(heads_pre[:, 2, :].reshape(count, H, HD))
    attended = lax.map(jax.checkpoint(row_attention), (query.reshape(rows, SEQ, H, HD), keys.reshape(rows, SEQ, H, HD), values.reshape(rows, SEQ, H, HD), ids))
    attended = low(low_back(attended.reshape(count, D)))
    branch = jnp.einsum('tc,ic->ti', attended, weights[:, 3, :], precision=highest)
    middle = inputs + low_back(branch) + vectors[4]
    later_norm = low(layer_norm(middle, vectors[2], vectors[3]))
    upper = jnp.einsum('td,drc->trc', later_norm, weights[:, 4:8, :], precision=highest) + vectors[9:13][None, :, :]
    upper = low_back(upper)
    hidden = low(quick_gelu(upper))
    mixed = jnp.einsum('trc,irc->ti', hidden, weights[:, 8:12, :], precision=highest)
    return middle + low_back(mixed) + vectors[5]

def reference(activations, cotangent, lengths, positions, weights, first_moment, second_moment, vectors, vector_first, vector_second):
    ids = picture_ids(lengths)
    cosine, sine = rotary_tables(positions)
    inputs = activations.astype(jnp.float32)

    def whole(inputs, weights, vectors):
        return forward(inputs, weights, vectors, ids, cosine, sine)
    result, pull = jax.vjp(whole, inputs, weights, vectors)
    input_grad, weight_grad, vector_grad = pull(cotangent.astype(jnp.float32))
    next_first, next_second, next_weights = adam_update(weights, weight_grad, first_moment, second_moment, rate_matrix, decay_matrix)
    next_vector_first, next_vector_second, next_vectors = adam_update(vectors, vector_grad, vector_first, vector_second, rate_vector, 0.0)
    return (result.astype(jnp.bfloat16), input_grad.astype(jnp.bfloat16), next_first, next_second, next_weights, next_vector_first, next_vector_second, next_vectors)
```

```python
import functools
import math

import jax
import jax.numpy as jnp
import numpy as np
from jax import lax
from jax.experimental import pallas as pl
from jax.experimental.pallas import tpu as pltpu
from jax.sharding import Mesh, PartitionSpec as P

HD = 80
LANES = 128
SEQ = 2048
STEP = 10
CHUNKS = 2

norm_eps = 1e-06
beta_first = 0.9
beta_second = 0.999
adam_eps = 1e-08
rate_matrix = 0.08
rate_vector = 0.6
decay_matrix = 0.05
gelu_slope = 1.702
masked_score = -1e30

LOW = jnp.bfloat16
FULL = jnp.float32
SQUARE = ("zl", "y")
LINE = ("zh", "zl")


def dot(a, b, dims):
    return lax.dot_general(a, b, (dims, ((), ())), preferred_element_type=FULL)


def nn(a, b):
    return dot(a, b, ((1,), (0,)))


def nt(a, b):
    return dot(a, b, ((1,), (1,)))


def tn(a, b):
    return dot(a, b, ((0,), (0,)))


def layer_norm(value, gain, shift):
    center = value - jnp.mean(value, axis=-1, keepdims=True)
    spread = jnp.mean(center * center, axis=-1, keepdims=True)
    return center * lax.rsqrt(spread + norm_eps) * gain + shift


def quick_gelu(value):
    return value * jax.nn.sigmoid(gelu_slope * value)


def adam_update(param, grad, first, second, rate, decay):
    first = beta_first * first + (1.0 - beta_first) * grad
    second = beta_second * second + (1.0 - beta_second) * grad * grad
    first_hat = first / (1.0 - beta_first**STEP)
    second_hat = second / (1.0 - beta_second**STEP)
    fresh = param - rate * (first_hat / (jnp.sqrt(second_hat) + adam_eps) + decay * param)
    return (first, second, fresh)


def swap(value, axis, far):
    return lax.ppermute(value, axis, [(i, i ^ far) for i in range(lax.axis_size(axis))])


def gather(value, axis):
    return [value] + [swap(value, axis, far) for far in range(1, lax.axis_size(axis))]


def settle(pieces, spot):
    bit = 1
    while bit < len(pieces):
        turned = (spot // bit) % 2 == 1
        pieces = [jnp.where(turned, pieces[i ^ bit], pieces[i]) for i in range(len(pieces))]
        bit *= 2
    return pieces


def scatter(value, axis, dim):
    spot = lax.axis_index(axis)

    def part(far):
        return lax.dynamic_index_in_dim(value, spot ^ far, dim, keepdims=False)

    total = part(0).astype(FULL)
    for far in range(1, lax.axis_size(axis)):
        total = total + swap(part(far).astype(LOW), axis, far).astype(FULL)
    return total


def scatter_near(pieces, axis):
    total = pieces[0].astype(FULL)
    for far in range(1, len(pieces)):
        total = total + swap(pieces[far].astype(LOW), axis, far).astype(FULL)
    return total


def leaves(things):
    return jax.tree.leaves(things)


def tie(value, *earlier):
    first = leaves(earlier)
    return pl.pallas_call(
        lambda *refs: None,
        in_specs=[pl.BlockSpec(memory_space=pl.ANY)] * (1 + len(first)),
        out_specs=pl.BlockSpec(memory_space=pl.ANY),
        out_shape=jax.ShapeDtypeStruct(value.shape, value.dtype),
        input_output_aliases={0: 0},
        name="tie",
    )(value, *first)


def sum_everywhere(value):
    for axis in ("c", "x", "y", "zl", "zh"):
        far = 1
        while far < lax.axis_size(axis):
            value = value + swap(value, axis, far)
            far *= 2
    return value


def project_kernel(heads, info_ref, rows_ref, w_ref, bias_ref, cos_ref, sin_ref, *refs):
    q_ref, k_ref, v_ref, kt_ref, vt_ref = refs[-5:]
    wide = heads * LANES
    cosine = cos_ref[...]
    sine = sin_ref[...]
    rows = rows_ref[...]
    factor = HD ** (-0.5) * math.log2(math.e)
    for slot in range(3):
        out = nn(rows, w_ref[:, slot * wide : (slot + 1) * wide])
        out = out + bias_ref[:, slot * wide : (slot + 1) * wide]
        for head in range(heads):
            lanes = slice(head * LANES, (head + 1) * LANES)
            value = out[:, lanes]
            if slot < 2:
                value = value * cosine + pltpu.roll(value, LANES // 2, 1) * sine
            if slot == 0:
                q_ref[:, lanes] = (value * factor).astype(LOW)
            elif slot == 1:
                k_ref[:, lanes] = value.astype(LOW)
                kt_ref[lanes, :] = value.T.astype(LOW)
            else:
                v_ref[:, lanes] = value.astype(LOW)
                vt_ref[lanes, :] = value.T.astype(LOW)


def project(info, rows, wide_w, wide_bias, cosine, sine, members, heads, earlier):
    total, width = rows.shape
    tile = total // (2 * members)
    wide = heads * LANES

    def place(g, info):
        return ((g % members) ^ info[0]) * 2 + g // members

    flat = pl.BlockSpec((tile, wide), lambda g, info: (place(g, info), 0))
    tall = pl.BlockSpec((wide, tile), lambda g, info: (0, place(g, info)))
    return pl.pallas_call(
        functools.partial(project_kernel, heads),
        grid_spec=pltpu.PrefetchScalarGridSpec(
            num_scalar_prefetch=1,
            grid=(2 * members,),
            in_specs=[
                pl.BlockSpec((tile, width), lambda g, info: (g, 0)),
                pl.BlockSpec((width, 3 * wide), lambda g, info: (0, 0)),
                pl.BlockSpec((1, 3 * wide), lambda g, info: (0, 0)),
                pl.BlockSpec((tile, LANES), lambda g, info: (g, 0)),
                pl.BlockSpec((tile, LANES), lambda g, info: (g, 0)),
            ]
            + [pl.BlockSpec(memory_space=pl.ANY)] * len(earlier),
            out_specs=[flat, flat, flat, tall, tall],
        ),
        out_shape=[jax.ShapeDtypeStruct((total, wide), LOW)] * 3
        + [jax.ShapeDtypeStruct((wide, total), LOW)] * 2,
        compiler_params=pltpu.CompilerParams(vmem_limit_bytes=48 << 20),
        cost_estimate=pl.CostEstimate(
            flops=2 * total * width * 3 * wide,
            bytes_accessed=2 * total * (width + 5 * wide) + 6 * width * wide,
            transcendentals=0,
        ),
        name="project",
    )(info, rows, wide_w, wide_bias, cosine, sine, *earlier)


def attend_kernel(heads, tile, info_ref, q_ref, k_ref, vt_ref, row_ids, column_ids, *refs):
    out_ref, lse_ref, acc_ref = refs[-3:]
    block = pl.program_id(0)
    first = info_ref[1 + block]
    last = info_ref[1 + pl.num_programs(0) + block]
    acc_ref[...] = jnp.zeros_like(acc_ref)
    mine = row_ids[0]

    def step(index, carry):
        start = pl.multiple_of(index * tile, tile)
        theirs = column_ids[pl.ds(start, tile), :]
        allowed = theirs == mine
        fresh = []
        for head in range(heads):
            lanes = slice(head * LANES, (head + 1) * LANES)
            top, summed = carry[head]
            scores = nt(k_ref[pl.ds(start, tile), lanes], q_ref[:, lanes])
            scores = jnp.where(allowed, scores, masked_score)
            higher = jnp.maximum(top, jnp.max(scores, axis=0, keepdims=True))
            shrink = jnp.exp2(top - higher)
            expo = jnp.exp2(scores - higher)
            summed = summed * shrink + jnp.sum(expo, axis=0, keepdims=True)
            part = nn(vt_ref[lanes, pl.ds(start, tile)], expo.astype(LOW))
            acc_ref[lanes, :] = acc_ref[lanes, :] * shrink + part
            fresh.append((higher, summed))
        return tuple(fresh)

    blank = (jnp.full((1, tile), masked_score, FULL), jnp.zeros((1, tile), FULL))
    done = lax.fori_loop(first, last, step, (blank,) * heads)
    for head in range(heads):
        lanes = slice(head * LANES, (head + 1) * LANES)
        top, summed = done[head]
        out_ref[:, lanes] = (acc_ref[lanes, :] / summed).T.astype(LOW)
        lse_ref[0, head : head + 1, :] = top + jnp.log2(summed)


def attend(info, query, keys, values_t, row_ids, column_ids, heads, group, earlier):
    total = query.shape[0]
    wide = heads * LANES
    blocks, _, tile = row_ids.shape

    return pl.pallas_call(
        functools.partial(attend_kernel, heads, tile),
        grid_spec=pltpu.PrefetchScalarGridSpec(
            num_scalar_prefetch=1,
            grid=(blocks,),
            in_specs=[
                pl.BlockSpec((tile, wide), lambda b, info: (b, group)),
                pl.BlockSpec((total, wide), lambda b, info: (0, group)),
                pl.BlockSpec((wide, total), lambda b, info: (group, 0)),
                pl.BlockSpec((1, 1, tile), lambda b, info: (b, 0, 0)),
                pl.BlockSpec((total, 1), lambda b, info: (0, 0)),
            ]
            + [pl.BlockSpec(memory_space=pl.ANY)] * len(earlier),
            out_specs=[
                pl.BlockSpec((tile, wide), lambda b, info: (b, 0)),
                pl.BlockSpec((1, heads, tile), lambda b, info: (b, 0, 0)),
            ],
            scratch_shapes=[pltpu.VMEM((wide, tile), FULL)],
        ),
        out_shape=[
            jax.ShapeDtypeStruct((total, wide), LOW),
            jax.ShapeDtypeStruct((blocks, heads, tile), FULL),
        ],
        compiler_params=pltpu.CompilerParams(vmem_limit_bytes=48 << 20),
        cost_estimate=pl.CostEstimate(
            flops=2 * total * total * wide, bytes_accessed=8 * total * wide, transcendentals=total * total * heads // 2
        ),
        name="attend",
    )(info, query, keys, values_t, row_ids, column_ids, *earlier)


def attend_back_kernel(
    heads,
    tile,
    members,
    info_ref,
    q_ref,
    k_ref,
    v_ref,
    kt_ref,
    do_ref,
    o_ref,
    lse_ref,
    row_ids,
    column_ids,
    cos_ref,
    sin_ref,
    *refs,
):
    out_ref, inner_ref, qt_ref, dk_ref, dv_ref = refs[-5:]
    block = pl.program_id(0)
    blocks = pl.num_programs(0)
    me = info_ref[0]
    first = info_ref[1 + block]
    last = info_ref[1 + blocks + block]
    wide = heads * LANES

    def place(b):
        return pl.multiple_of(b * tile, tile)

    def home(b):
        return pl.multiple_of(((b % 2) * members + ((b // 2) ^ me)) * tile, tile)

    def unrotate(value, b):
        where = pl.ds(home(b), tile)
        return value * cos_ref[where, :] - pltpu.roll(value, LANES // 2, 1) * sin_ref[where, :]

    @pl.when(block == 0)
    def _():
        qt_ref[...] = jnp.zeros_like(qt_ref)

        def fill(b, carry):
            where = pl.ds(place(b), tile)
            for head in range(heads):
                lanes = slice(head * LANES, (head + 1) * LANES)
                both = o_ref[where, lanes].astype(FULL) * do_ref[where, lanes].astype(FULL)
                inner_ref[b, head : head + 1, :] = jnp.sum(both.T, axis=0, keepdims=True)
            return carry

        lax.fori_loop(0, blocks, fill, 0)

    dk_ref[...] = jnp.zeros_like(dk_ref)
    dv_ref[...] = jnp.zeros_like(dv_ref)
    here = pl.ds(place(block), tile)
    theirs = column_ids[pl.ds(pl.multiple_of(block * tile, tile), tile), :]

    def step(index, carry):
        where = pl.ds(place(index), tile)
        allowed = theirs == row_ids[index]
        for head in range(heads):
            lanes = slice(head * LANES, (head + 1) * LANES)
            query = q_ref[where, lanes]
            grad = do_ref[where, lanes]
            scores = nt(k_ref[here, lanes], query)
            scores = jnp.where(allowed, scores, masked_score)
            probs = jnp.exp2(scores - lse_ref[index, head : head + 1, :])
            prob_grad = nt(v_ref[here, lanes], grad)
            score_grad = (probs * (prob_grad - inner_ref[index, head : head + 1, :])).astype(LOW)
            dv_ref[:, lanes] += nn(probs.astype(LOW), grad)
            dk_ref[:, lanes] += nn(score_grad, query)
            qt_ref[lanes, where] += nn(kt_ref[lanes, here], score_grad)
        return carry

    lax.fori_loop(first, last, step, 0)
    rows = pl.ds(home(block), tile)
    for head in range(heads):
        lanes = slice(head * LANES, (head + 1) * LANES)
        key_grad = unrotate(dk_ref[:, lanes] * math.log(2.0), block)
        out_ref[rows, wide + head * LANES : wide + (head + 1) * LANES] = key_grad.astype(LOW)
        out_ref[rows, 2 * wide + head * LANES : 2 * wide + (head + 1) * LANES] = dv_ref[:, lanes].astype(LOW)

    @pl.when(block == blocks - 1)
    def _():
        def spill(b, carry):
            for head in range(heads):
                lanes = slice(head * LANES, (head + 1) * LANES)
                query_grad = qt_ref[lanes, pl.ds(place(b), tile)].T * HD ** (-0.5)
                out_ref[pl.ds(home(b), tile), lanes] = unrotate(query_grad, b).astype(LOW)
            return carry

        lax.fori_loop(0, blocks, spill, 0)


def attend_back(info, query, keys, values, keys_t, grad, attended, logs, row_ids, column_ids, cosine, sine, members, heads, group, earlier):
    total = query.shape[0]
    wide = heads * LANES
    blocks, _, tile = row_ids.shape

    def whole(*shape):
        return pl.BlockSpec(shape, lambda b, info: (0,) * len(shape), pipeline_mode=pl.Buffered(1))

    flat = pl.BlockSpec((total, wide), lambda b, info: (0, group), pipeline_mode=pl.Buffered(1))
    tall = pl.BlockSpec((wide, total), lambda b, info: (group, 0), pipeline_mode=pl.Buffered(1))

    return pl.pallas_call(
        functools.partial(attend_back_kernel, heads, tile, members),
        grid_spec=pltpu.PrefetchScalarGridSpec(
            num_scalar_prefetch=1,
            grid=(blocks,),
            in_specs=[
                flat,
                flat,
                flat,
                tall,
                flat,
                whole(total, wide),
                whole(blocks, heads, tile),
                whole(blocks, 1, tile),
                whole(total, 1),
                whole(total, LANES),
                whole(total, LANES),
            ]
            + [pl.BlockSpec(memory_space=pl.ANY)] * len(earlier),
            out_specs=whole(total, 3 * wide),
            scratch_shapes=[
                pltpu.VMEM((blocks, heads, tile), FULL),
                pltpu.VMEM((wide, total), FULL),
                pltpu.VMEM((tile, wide), FULL),
                pltpu.VMEM((tile, wide), FULL),
            ],
        ),
        out_shape=jax.ShapeDtypeStruct((total, 3 * wide), LOW),
        compiler_params=pltpu.CompilerParams(vmem_limit_bytes=56 << 20),
        cost_estimate=pl.CostEstimate(
            flops=5 * total * total * wide, bytes_accessed=18 * total * wide, transcendentals=total * total * heads // 2
        ),
        name="attend_back",
    )(
        info, query, keys, values, keys_t, grad, attended, logs, row_ids, column_ids, cosine, sine, *earlier
    )


def spread_matrix(shards, slots, heads_each, turned):
    heads = shards * heads_each
    out = np.zeros((shards, slots, heads_each, HD, slots, heads, LANES), np.float32)
    half = HD // 2
    for shard in range(shards):
        for slot in range(slots):
            for head in range(heads_each):
                for j in range(HD):
                    lane = j
                    if turned and slot < 2 and j >= half:
                        lane = LANES // 2 + j - half
                    out[shard, slot, head, j, slot, shard * heads_each + head, lane] = 1.0
    return out.reshape(shards * slots * heads_each * HD, slots * heads * LANES)


def local(
    activations,
    cotangent,
    lengths,
    positions,
    weights,
    first_moment,
    second_moment,
    vectors,
    vector_first,
    vector_second,
):
    tokens, width = activations.shape
    depth, slots, columns = weights.shape
    half = tokens // 2
    shards = lax.axis_size("zh")
    ys = lax.axis_size("y")
    xs = lax.axis_size("x")
    members = 2 * ys
    heads_each = columns // HD
    heads = shards * heads_each
    x, c, zh, zl, y = (lax.axis_index(a) for a in ("x", "c", "zh", "zl", "y"))
    me = zl * ys + y
    members_of = shards * members
    four = 4 * columns
    everyone = ("zh", "zl", "y", "x", "c")

    inputs = activations.astype(FULL)
    early_norm = layer_norm(inputs, vectors[0], vectors[1]).astype(LOW)

    low = weights.astype(LOW)
    lift = jnp.concatenate([low[:, 4:8, :].reshape(depth, four), low[:, 3, :]], axis=1)
    down = low[:, 8:12, :].reshape(depth, four)
    lift_all = lax.all_gather(lift, everyone, axis=0, tiled=True)
    lift_all = lift_all.reshape(members_of, width, four + columns)
    down_w = lax.all_gather(down, everyone, axis=0, tiled=True)
    down_w = down_w.reshape(members_of, width, four)
    lift_w = lift_all[:, :, :four]
    out_w = jnp.concatenate(
        [lift_all[h * members + m, :, four:] for m in range(members) for h in range(shards)], axis=1
    )

    part = jnp.concatenate(gather(early_norm[:half], "y"), axis=0)
    rows_a = jnp.concatenate(gather(part, "zl"), axis=0)
    part = jnp.concatenate(gather(early_norm[half:], "zl"), axis=0).reshape(2, half, width)
    rows_b = jnp.stack(gather(part, "y"), axis=1).reshape(members * half, width)
    early_rows = jnp.concatenate([rows_a, rows_b], axis=0)

    qkv = low[:, 0:3, :].reshape(depth, 3 * columns)
    qkv = jnp.concatenate(settle(gather(qkv, "zh"), zh), axis=1)
    qkv = jnp.stack(settle(gather(qkv, "x"), x), axis=0)
    qkv = jnp.stack(settle(gather(qkv, "c"), c), axis=1).reshape(width, shards * 3 * columns)
    spread = spread_matrix(shards, 3, heads_each, True)
    spread_low = jnp.asarray(spread, LOW)
    wide_w = nn(qkv, spread_low).astype(LOW)
    shard_of = jnp.arange(shards) * members + me
    qkv_bias = jnp.take(vectors[6:9].reshape(3, -1, columns), shard_of, axis=1)
    qkv_bias = jnp.swapaxes(qkv_bias, 0, 1).reshape(1, -1)
    wide_bias = lax.dot(qkv_bias, jnp.asarray(spread), precision=lax.Precision.HIGHEST)

    counts = lax.dynamic_index_in_dim(lengths, zh, 0, keepdims=False)
    ends = jnp.cumsum(counts)
    spots = jnp.arange(SEQ, dtype=jnp.int32)
    ids = jnp.sum((spots[:, None] >= ends[None, :]).astype(jnp.int32), axis=1)
    blocks = 2 * members
    id_blocks = ids.reshape(blocks, half)
    low_spot = jnp.sum((ids[None, :] < id_blocks[:, :1]).astype(jnp.int32), axis=1)
    high_spot = jnp.sum((ids[None, :] <= id_blocks[:, -1:]).astype(jnp.int32), axis=1)
    info = jnp.concatenate(
        [me.reshape(1).astype(jnp.int32), low_spot // half, (high_spot + half - 1) // half]
    ).astype(jnp.int32)
    row_ids = ids.reshape(blocks, 1, half)
    column_ids = ids.reshape(SEQ, 1)

    spot = lax.dynamic_slice_in_dim(positions, zh * SEQ, SEQ, 1).reshape(2, members, 2, half)
    spot = jnp.take(spot, me ^ jnp.arange(members), axis=1)
    spot = jnp.swapaxes(spot, 1, 2).reshape(2, SEQ).astype(FULL)
    quarter = HD // 4
    freq = 10000.0 ** (-jnp.arange(quarter, dtype=FULL) * 4.0 / HD)
    angle = jnp.concatenate([spot[0][:, None] * freq, spot[1][:, None] * freq], axis=1)
    cosine, sine = jnp.cos(angle), jnp.sin(angle)
    gap = jnp.zeros((SEQ, LANES // 2 - HD // 2), FULL)
    cosine = jnp.concatenate([cosine, gap, cosine, gap], axis=1)
    sine = jnp.concatenate([-sine, gap, sine, gap], axis=1)

    query, keys, values, keys_t, values_t = project(
        info, early_rows, wide_w, wide_bias, cosine, sine, members, heads, []
    )
    groups = 2
    few = heads // groups
    attended_wide, logs = [], []
    for group in range(groups):
        some, log = attend(
            info, query, keys, values_t, row_ids, column_ids, few, group, logs[:1]
        )
        attended_wide.append(some)
        logs.append(log)

    squeeze = jnp.asarray(spread_matrix(shards, 1, heads_each, False).T, LOW)
    own = nn(attended_wide[0], squeeze[: few * LANES]) + nn(attended_wide[1], squeeze[few * LANES :])
    own = own.astype(LOW).reshape(members, tokens, shards * columns)
    own = lax.all_to_all(own, SQUARE, split_axis=0, concat_axis=0, tiled=True)
    attended = jnp.swapaxes(own, 0, 1).reshape(tokens, width)

    middle = inputs + nt(attended, out_w) + vectors[4]
    later_norm = layer_norm(middle, vectors[2], vectors[3]).astype(LOW)

    lift_bias = jnp.swapaxes(vectors[9:13].reshape(4, members_of, columns), 0, 1)
    lift_bias = lift_bias.reshape(members_of, 1, four)
    upper = jnp.einsum("nd,tdj->tnj", later_norm, lift_w, preferred_element_type=FULL) + lift_bias
    hidden = quick_gelu(upper).astype(LOW)

    mixed = jnp.einsum("tnj,tij->ni", hidden, down_w, preferred_element_type=FULL)
    block_output = (middle + mixed + vectors[5]).astype(LOW)

    def split(value):
        value = value.reshape(tokens, xs, 2, depth)
        parts = [value[:, :, i].reshape(tokens, xs * depth) for i in range(2)]
        return jnp.where(c == 0, parts[0], parts[1]), jnp.where(c == 0, parts[1], parts[0])

    def first_sum(left, right):
        mine, theirs = left
        theirs = jnp.einsum("ni,tnj->tij", theirs, right, preferred_element_type=FULL)
        theirs = swap(theirs.astype(LOW), "c", 1).astype(FULL)
        mine = jnp.einsum("ni,tnj->tij", mine, right, preferred_element_type=FULL)
        return (mine + theirs).astype(LOW)

    step = depth // CHUNKS

    def chunk(value, k):
        value = value.reshape(2 * shards, ys, xs, CHUNKS, step, value.shape[-1])
        return value[:, :, :, k]

    def over_plane(value, order):
        first = scatter(value, order[0], 1 if order[0] == "y" else 2).astype(LOW)
        last = scatter(first, order[1], 1).astype(LOW)
        return first, last

    cot_parts = split(cotangent)
    down_sum = first_sum(cot_parts, hidden)
    down_plane = [over_plane(chunk(down_sum, 0), "yx"), over_plane(chunk(down_sum, 1), "xy")]
    down_grad = jnp.concatenate([scatter(last, LINE, 0) for _, last in down_plane], axis=0)

    hidden_grad = jnp.einsum("ni,tij->tnj", cotangent, down_w, preferred_element_type=FULL)
    upper_grad = jax.vjp(quick_gelu, upper)[1](hidden_grad)[0].astype(LOW)
    lift_sum = first_sum(split(later_norm), upper_grad)
    lift_plane = [over_plane(chunk(lift_sum, 0), "xy"), over_plane(chunk(lift_sum, 1), "xy")]
    lift_grad = jnp.concatenate([scatter(last, LINE, 0) for _, last in lift_plane], axis=0)

    later_grad = jnp.einsum("tnj,tdj->nd", upper_grad, lift_w, preferred_element_type=FULL)

    cot_full = cotangent.astype(FULL)
    middle_part, gain_second, shift_second = jax.vjp(layer_norm, middle, vectors[2], vectors[3])[1](
        later_grad
    )
    middle_grad = cot_full + middle_part
    middle_low = tie(middle_grad.astype(LOW), [first for first, _ in down_plane])

    attended_grad = nn(middle_low, out_w).astype(LOW)
    row_grad = jnp.swapaxes(attended_grad.reshape(tokens, members, shards * columns), 0, 1)
    row_grad = lax.all_to_all(row_grad, SQUARE, split_axis=0, concat_axis=0, tiled=True)
    row_grad = nt(row_grad.reshape(SEQ, shards * columns), squeeze).astype(LOW)

    mine, theirs = split(middle_low)
    out_sum = (tn(mine, attended) + swap(tn(theirs, attended).astype(LOW), "c", 1).astype(FULL)).astype(LOW)
    out_sum = scatter(out_sum.reshape(xs, depth, width), "x", 0).astype(LOW)
    out_sum = out_sum.reshape(depth, 2, ys, shards, columns)
    out_sum = jnp.moveaxis(out_sum, (3, 1, 2), (0, 1, 2)).reshape(2 * shards, ys, depth, columns)
    out_sum = scatter(out_sum, "y", 1).astype(LOW)
    out_grad = scatter(out_sum, LINE, 0)

    heads_grad = []
    waits = [
        leaves((lift_plane[0][0], [last for _, last in down_plane])),
        leaves((lift_plane[1][0], down_grad)),
    ]
    for group in range(groups):
        heads_grad.append(
            attend_back(
                info,
                query,
                keys,
                values,
                keys_t,
                row_grad,
                attended_wide[group],
                logs[group],
                row_ids,
                column_ids,
                cosine,
                sine,
                members,
                few,
                group,
                waits[group] + heads_grad[:1],
            )
        )
    pack = spread_low.reshape(-1, 3, groups, few * LANES)
    pack = [pack[:, :, group].reshape(-1, 3 * few * LANES) for group in range(groups)]
    heads_grad = (nt(heads_grad[0], pack[0]) + nt(heads_grad[1], pack[1])).astype(LOW)
    heads_grad = tie(heads_grad, [last for _, last in lift_plane])

    partial = nt(heads_grad, qkv).astype(LOW).reshape(2, 2, ys, half, width)
    some = scatter_near([partial[0, l] for l in range(2)], "zl")
    some_a = scatter_near([some[j] for j in range(ys)], "y")
    some = scatter_near([partial[1, :, j] for j in range(ys)], "y")
    some_b = scatter_near([some[l] for l in range(2)], "zl")
    early_grad = jnp.concatenate([some_a, some_b], axis=0)

    qkv_grad = tn(early_rows, heads_grad).astype(LOW).reshape(xs, 2, depth, shards * 3 * columns)
    qkv_grad = scatter(qkv_grad, "c", 1).astype(LOW)
    qkv_grad = scatter(qkv_grad, "x", 0).astype(LOW)
    qkv_grad = jnp.swapaxes(qkv_grad.reshape(depth, shards, 3 * columns), 0, 1)
    qkv_grad = scatter(qkv_grad, "zh", 0)

    input_part, gain_first, shift_first = jax.vjp(layer_norm, inputs, vectors[0], vectors[1])[1](
        early_grad
    )
    input_grad = (middle_grad + input_part).astype(LOW)

    owned = jnp.concatenate([qkv_grad, out_grad, lift_grad, down_grad], axis=1)
    owned = owned.reshape(depth, slots, columns)

    ffn_sum = jnp.sum(upper_grad, axis=1, dtype=FULL).reshape(members_of, 4, columns)
    ffn_bias = jnp.swapaxes(ffn_sum, 0, 1).reshape(4, width)
    ready = jnp.stack(
        [gain_second, shift_second, jnp.sum(middle_grad, axis=0), jnp.sum(cot_full, axis=0)]
    )
    ready = sum_everywhere(jnp.concatenate([ready, ffn_bias], axis=0))
    heads_sum = jnp.sum(heads_grad, axis=0, dtype=FULL).reshape(shards, 3, columns)
    placed = jnp.where(
        (jnp.arange(members) == me)[None, None, :, None],
        jnp.swapaxes(heads_sum, 0, 1)[:, :, None, :],
        0.0,
    ).reshape(3, width)
    late = sum_everywhere(jnp.concatenate([jnp.stack([gain_first, shift_first]), placed], axis=0))
    vector_grad = jnp.concatenate([late[0:2], ready[0:4], late[2:5], ready[4:8]], axis=0)

    next_first, next_second, next_weights = adam_update(
        weights, owned, first_moment, second_moment, rate_matrix, decay_matrix
    )
    next_vector_first, next_vector_second, next_vectors = adam_update(
        vectors, vector_grad, vector_first, vector_second, rate_vector, 0.0
    )
    return (
        block_output,
        input_grad,
        next_first,
        next_second,
        next_weights,
        next_vector_first,
        next_vector_second,
        next_vectors,
    )


def solution(mesh):
    fsdp = mesh.shape["fsdp"]
    tp = mesh.shape["tp"]
    outer = ("x", "c")
    inner = ("zh", "zl", "y")

    def run(*args):
        rows = args[2].shape[0] // fsdp
        fine = Mesh(
            mesh.devices.reshape(fsdp // 2, 2, rows, 2, tp // (2 * rows)), outer + inner
        )
        patches = P(outer + inner, None)
        matrix = P(outer, None, inner)
        in_specs = (
            patches,
            patches,
            P(outer, None),
            P(None, outer),
            matrix,
            matrix,
            matrix,
            P(),
            P(),
            P(),
        )
        out_specs = (patches, patches, matrix, matrix, matrix, P(), P(), P())
        return jax.shard_map(
            local, mesh=fine, in_specs=in_specs, out_specs=out_specs, check_vma=False
        )(*args)

    return run
```

```python
import functools
import math

import jax
import jax.numpy as jnp
import numpy as np
from jax import lax
from jax.experimental import pallas as pl
from jax.experimental.pallas import tpu as pltpu
from jax.sharding import Mesh, PartitionSpec as P

HD = 80
LANES = 128
SEQ = 2048
STEP = 10
CHUNKS = 2

norm_eps = 1e-06
beta_first = 0.9
beta_second = 0.999
adam_eps = 1e-08
rate_matrix = 0.08
rate_vector = 0.6
decay_matrix = 0.05
gelu_slope = 1.702
masked_score = -1e30

LOW = jnp.bfloat16
FULL = jnp.float32
SQUARE = ("zl", "y")
LINE = ("zh", "zl")


def dot(a, b, dims):
    return lax.dot_general(a, b, (dims, ((), ())), preferred_element_type=FULL)


def nn(a, b):
    return dot(a, b, ((1,), (0,)))


def nt(a, b):
    return dot(a, b, ((1,), (1,)))


def tn(a, b):
    return dot(a, b, ((0,), (0,)))


def layer_norm(value, gain, shift):
    center = value - jnp.mean(value, axis=-1, keepdims=True)
    spread = jnp.mean(center * center, axis=-1, keepdims=True)
    return center * lax.rsqrt(spread + norm_eps) * gain + shift


def quick_gelu(value):
    return value * jax.nn.sigmoid(gelu_slope * value)


def adam_update(param, grad, first, second, rate, decay):
    first = beta_first * first + (1.0 - beta_first) * grad
    second = beta_second * second + (1.0 - beta_second) * grad * grad
    first_hat = first / (1.0 - beta_first**STEP)
    second_hat = second / (1.0 - beta_second**STEP)
    fresh = param - rate * (first_hat / (jnp.sqrt(second_hat) + adam_eps) + decay * param)
    return (first, second, fresh)


def swap(value, axis, far):
    return lax.ppermute(value, axis, [(i, i ^ far) for i in range(lax.axis_size(axis))])


def gather(value, axis):
    return [value] + [swap(value, axis, far) for far in range(1, lax.axis_size(axis))]


def settle(pieces, spot):
    bit = 1
    while bit < len(pieces):
        turned = (spot // bit) % 2 == 1
        pieces = [jnp.where(turned, pieces[i ^ bit], pieces[i]) for i in range(len(pieces))]
        bit *= 2
    return pieces


def scatter(value, axis, dim):
    spot = lax.axis_index(axis)

    def part(far):
        return lax.dynamic_index_in_dim(value, spot ^ far, dim, keepdims=False)

    total = part(0).astype(FULL)
    for far in range(1, lax.axis_size(axis)):
        total = total + swap(part(far).astype(LOW), axis, far).astype(FULL)
    return total


def scatter_near(pieces, axis):
    total = pieces[0].astype(FULL)
    for far in range(1, len(pieces)):
        total = total + swap(pieces[far].astype(LOW), axis, far).astype(FULL)
    return total


def leaves(things):
    return jax.tree.leaves(things)


def tie(value, *earlier):
    first = leaves(earlier)
    return pl.pallas_call(
        lambda *refs: None,
        in_specs=[pl.BlockSpec(memory_space=pl.ANY)] * (1 + len(first)),
        out_specs=pl.BlockSpec(memory_space=pl.ANY),
        out_shape=jax.ShapeDtypeStruct(value.shape, value.dtype),
        input_output_aliases={0: 0},
        name="tie",
    )(value, *first)


def sum_everywhere(value):
    for axis in ("c", "x", "y", "zl", "zh"):
        far = 1
        while far < lax.axis_size(axis):
            value = value + swap(value, axis, far)
            far *= 2
    return value


def project_kernel(heads, info_ref, rows_ref, w_ref, bias_ref, cos_ref, sin_ref, *refs):
    q_ref, k_ref, v_ref, kt_ref, vt_ref = refs[-5:]
    wide = heads * LANES
    cosine = cos_ref[...]
    sine = sin_ref[...]
    rows = rows_ref[...]
    factor = HD ** (-0.5) * math.log2(math.e)
    for slot in range(3):
        out = nn(rows, w_ref[:, slot * wide : (slot + 1) * wide])
        out = out + bias_ref[:, slot * wide : (slot + 1) * wide]
        for head in range(heads):
            lanes = slice(head * LANES, (head + 1) * LANES)
            value = out[:, lanes]
            if slot < 2:
                value = value * cosine + pltpu.roll(value, LANES // 2, 1) * sine
            if slot == 0:
                q_ref[:, lanes] = (value * factor).astype(LOW)
            elif slot == 1:
                k_ref[:, lanes] = value.astype(LOW)
                kt_ref[lanes, :] = value.T.astype(LOW)
            else:
                v_ref[:, lanes] = value.astype(LOW)
                vt_ref[lanes, :] = value.T.astype(LOW)


def project(info, rows, wide_w, wide_bias, cosine, sine, members, heads, earlier):
    total, width = rows.shape
    tile = total // (2 * members)
    wide = heads * LANES

    def place(g, info):
        return ((g % members) ^ info[0]) * 2 + g // members

    flat = pl.BlockSpec((tile, wide), lambda g, info: (place(g, info), 0))
    tall = pl.BlockSpec((wide, tile), lambda g, info: (0, place(g, info)))
    return pl.pallas_call(
        functools.partial(project_kernel, heads),
        grid_spec=pltpu.PrefetchScalarGridSpec(
            num_scalar_prefetch=1,
            grid=(2 * members,),
            in_specs=[
                pl.BlockSpec((tile, width), lambda g, info: (g, 0)),
                pl.BlockSpec((width, 3 * wide), lambda g, info: (0, 0)),
                pl.BlockSpec((1, 3 * wide), lambda g, info: (0, 0)),
                pl.BlockSpec((tile, LANES), lambda g, info: (g, 0)),
                pl.BlockSpec((tile, LANES), lambda g, info: (g, 0)),
            ]
            + [pl.BlockSpec(memory_space=pl.ANY)] * len(earlier),
            out_specs=[flat, flat, flat, tall, tall],
        ),
        out_shape=[jax.ShapeDtypeStruct((total, wide), LOW)] * 3
        + [jax.ShapeDtypeStruct((wide, total), LOW)] * 2,
        compiler_params=pltpu.CompilerParams(vmem_limit_bytes=48 << 20),
        cost_estimate=pl.CostEstimate(
            flops=2 * total * width * 3 * wide,
            bytes_accessed=2 * total * (width + 5 * wide) + 6 * width * wide,
            transcendentals=0,
        ),
        name="project",
    )(info, rows, wide_w, wide_bias, cosine, sine, *earlier)


def attend_kernel(heads, tile, info_ref, q_ref, k_ref, vt_ref, row_ids, column_ids, pack_ref, *refs):
    out_ref, lse_ref, acc_ref = refs[-3:]
    block = pl.program_id(0)
    first = info_ref[1 + block]
    last = info_ref[1 + pl.num_programs(0) + block]
    acc_ref[...] = jnp.zeros_like(acc_ref)
    mine = row_ids[0]

    def step(index, carry):
        start = pl.multiple_of(index * tile, tile)
        theirs = column_ids[pl.ds(start, tile), :]
        allowed = theirs == mine
        fresh = []
        for head in range(heads):
            lanes = slice(head * LANES, (head + 1) * LANES)
            top, summed = carry[head]
            scores = nt(k_ref[pl.ds(start, tile), lanes], q_ref[:, lanes])
            scores = jnp.where(allowed, scores, masked_score)
            higher = jnp.maximum(top, jnp.max(scores, axis=0, keepdims=True))
            shrink = jnp.exp2(top - higher)
            expo = jnp.exp2(scores - higher)
            summed = summed * shrink + jnp.sum(expo, axis=0, keepdims=True)
            part = nn(vt_ref[lanes, pl.ds(start, tile)], expo.astype(LOW))
            acc_ref[lanes, :] = acc_ref[lanes, :] * shrink + part
            fresh.append((higher, summed))
        return tuple(fresh)

    blank = (jnp.full((1, tile), masked_score, FULL), jnp.zeros((1, tile), FULL))
    done = lax.fori_loop(first, last, step, (blank,) * heads)
    for head in range(heads):
        lanes = slice(head * LANES, (head + 1) * LANES)
        top, summed = done[head]
        acc_ref[lanes, :] = acc_ref[lanes, :] / summed
        lse_ref[0, head : head + 1, :] = top + jnp.log2(summed)
    out_ref[...] = tn(acc_ref[...].astype(LOW), pack_ref[...]).astype(LOW)


def attend(info, query, keys, values_t, row_ids, column_ids, pack, heads, group, earlier):
    total = query.shape[0]
    wide = heads * LANES
    blocks, _, tile = row_ids.shape

    return pl.pallas_call(
        functools.partial(attend_kernel, heads, tile),
        grid_spec=pltpu.PrefetchScalarGridSpec(
            num_scalar_prefetch=1,
            grid=(blocks,),
            in_specs=[
                pl.BlockSpec((tile, wide), lambda b, info: (b, group)),
                pl.BlockSpec((total, wide), lambda b, info: (0, group)),
                pl.BlockSpec((wide, total), lambda b, info: (group, 0)),
                pl.BlockSpec((1, 1, tile), lambda b, info: (b, 0, 0)),
                pl.BlockSpec((total, 1), lambda b, info: (0, 0)),
                pl.BlockSpec(pack.shape, lambda b, info: (0, 0)),
            ]
            + [pl.BlockSpec(memory_space=pl.ANY)] * len(earlier),
            out_specs=[
                pl.BlockSpec((tile, heads * HD), lambda b, info: (b, 0)),
                pl.BlockSpec((1, heads, tile), lambda b, info: (b, 0, 0)),
            ],
            scratch_shapes=[pltpu.VMEM((wide, tile), FULL)],
        ),
        out_shape=[
            jax.ShapeDtypeStruct((total, heads * HD), LOW),
            jax.ShapeDtypeStruct((blocks, heads, tile), FULL),
        ],
        compiler_params=pltpu.CompilerParams(vmem_limit_bytes=48 << 20),
        cost_estimate=pl.CostEstimate(
            flops=2 * total * total * wide, bytes_accessed=8 * total * wide, transcendentals=total * total * heads // 2
        ),
        name="attend",
    )(info, query, keys, values_t, row_ids, column_ids, pack, *earlier)


def attend_back_kernel(
    heads,
    tile,
    members,
    info_ref,
    q_ref,
    k_ref,
    v_ref,
    kt_ref,
    grad_ref,
    o_ref,
    lse_ref,
    row_ids,
    column_ids,
    cos_ref,
    sin_ref,
    pack_ref,
    spread_ref,
    *refs,
):
    out_ref, inner_ref, do_ref, qt_ref, dk_ref, dv_ref = refs[-6:]
    block = pl.program_id(0)
    blocks = pl.num_programs(0)
    me = info_ref[0]
    first = info_ref[1 + block]
    last = info_ref[1 + blocks + block]
    wide = heads * LANES

    def place(b):
        return pl.multiple_of(b * tile, tile)

    def home(b):
        return pl.multiple_of(((b % 2) * members + ((b // 2) ^ me)) * tile, tile)

    def unrotate(value, b):
        where = pl.ds(home(b), tile)
        return value * cos_ref[where, :] - pltpu.roll(value, LANES // 2, 1) * sin_ref[where, :]

    @pl.when(block == 0)
    def _():
        qt_ref[...] = jnp.zeros_like(qt_ref)

        lane = lax.broadcasted_iota(jnp.int32, (8, heads * HD), 1)
        head = lax.broadcasted_iota(jnp.int32, (8, heads * HD), 0)
        pick = ((lane >= head * HD) & (lane < (head + 1) * HD)).astype(FULL)

        def fill(b, carry):
            where = pl.ds(place(b), tile)
            grad = grad_ref[where, :]
            do_ref[where, :] = nt(grad, pack_ref[...]).astype(LOW)
            both = o_ref[where, :].astype(FULL) * grad.astype(FULL)
            inner_ref[b] = lax.dot_general(
                pick,
                both,
                (((1,), (1,)), ((), ())),
                precision=lax.Precision.HIGHEST,
                preferred_element_type=FULL,
            )
            return carry

        lax.fori_loop(0, blocks, fill, 0)

    dk_ref[...] = jnp.zeros_like(dk_ref)
    dv_ref[...] = jnp.zeros_like(dv_ref)
    here = pl.ds(place(block), tile)
    theirs = column_ids[pl.ds(pl.multiple_of(block * tile, tile), tile), :]

    def step(index, carry):
        where = pl.ds(place(index), tile)
        allowed = theirs == row_ids[index]
        for head in range(heads):
            lanes = slice(head * LANES, (head + 1) * LANES)
            query = q_ref[where, lanes]
            grad = do_ref[where, lanes]
            scores = nt(k_ref[here, lanes], query)
            scores = jnp.where(allowed, scores, masked_score)
            probs = jnp.exp2(scores - lse_ref[index, head : head + 1, :])
            prob_grad = nt(v_ref[here, lanes], grad)
            score_grad = (probs * (prob_grad - inner_ref[index, head : head + 1, :])).astype(LOW)
            dv_ref[:, lanes] += nn(probs.astype(LOW), grad)
            dk_ref[:, lanes] += nn(score_grad, query)
            qt_ref[lanes, where] += nn(kt_ref[lanes, here], score_grad)
        return carry

    lax.fori_loop(first, last, step, 0)
    rows = pl.ds(home(block), tile)
    for head in range(heads):
        lanes = slice(head * LANES, (head + 1) * LANES)
        dk_ref[:, lanes] = unrotate(dk_ref[:, lanes] * math.log(2.0), block)
    key_part = nt(dk_ref[...].astype(LOW), spread_ref[:, wide : 2 * wide])
    value_part = nt(dv_ref[...].astype(LOW), spread_ref[:, 2 * wide :])
    out_ref[rows, :] = (key_part + value_part).astype(LOW)

    @pl.when(block == blocks - 1)
    def _():
        def spill(b, carry):
            rows = pl.ds(home(b), tile)
            for head in range(heads):
                lanes = slice(head * LANES, (head + 1) * LANES)
                query_grad = qt_ref[lanes, pl.ds(place(b), tile)].T * HD ** (-0.5)
                dk_ref[:, lanes] = unrotate(query_grad, b)
            query_part = nt(dk_ref[...].astype(LOW), spread_ref[:, :wide])
            out_ref[rows, :] = (out_ref[rows, :].astype(FULL) + query_part).astype(LOW)
            return carry

        lax.fori_loop(0, blocks, spill, 0)


def attend_back(info, query, keys, values, keys_t, grad, attended, logs, row_ids, column_ids, cosine, sine, pack, spread, members, heads, group, earlier):
    total = query.shape[0]
    wide = heads * LANES
    blocks, _, tile = row_ids.shape

    def whole(*shape):
        return pl.BlockSpec(shape, lambda b, info: (0,) * len(shape), pipeline_mode=pl.Buffered(1))

    flat = pl.BlockSpec((total, wide), lambda b, info: (0, group), pipeline_mode=pl.Buffered(1))
    tall = pl.BlockSpec((wide, total), lambda b, info: (group, 0), pipeline_mode=pl.Buffered(1))

    return pl.pallas_call(
        functools.partial(attend_back_kernel, heads, tile, members),
        grid_spec=pltpu.PrefetchScalarGridSpec(
            num_scalar_prefetch=1,
            grid=(blocks,),
            in_specs=[
                flat,
                flat,
                flat,
                tall,
                whole(total, heads * HD),
                whole(total, heads * HD),
                whole(blocks, heads, tile),
                whole(blocks, 1, tile),
                whole(total, 1),
                whole(total, LANES),
                whole(total, LANES),
                whole(*pack.shape),
                whole(*spread.shape),
            ]
            + [pl.BlockSpec(memory_space=pl.ANY)] * len(earlier),
            out_specs=whole(total, 3 * heads * HD),
            scratch_shapes=[
                pltpu.VMEM((blocks, 8, tile), FULL),
                pltpu.VMEM((total, wide), LOW),
                pltpu.VMEM((wide, total), FULL),
                pltpu.VMEM((tile, wide), FULL),
                pltpu.VMEM((tile, wide), FULL),
            ],
        ),
        out_shape=jax.ShapeDtypeStruct((total, 3 * heads * HD), LOW),
        compiler_params=pltpu.CompilerParams(vmem_limit_bytes=56 << 20),
        cost_estimate=pl.CostEstimate(
            flops=5 * total * total * wide, bytes_accessed=18 * total * wide, transcendentals=total * total * heads // 2
        ),
        name="attend_back",
    )(
        info,
        query,
        keys,
        values,
        keys_t,
        grad,
        attended,
        logs,
        row_ids,
        column_ids,
        cosine,
        sine,
        pack,
        spread,
        *earlier,
    )


def spread_matrix(shards, slots, heads_each, turned):
    heads = shards * heads_each
    out = np.zeros((shards, slots, heads_each, HD, slots, heads, LANES), np.float32)
    half = HD // 2
    for shard in range(shards):
        for slot in range(slots):
            for head in range(heads_each):
                for j in range(HD):
                    lane = j
                    if turned and slot < 2 and j >= half:
                        lane = LANES // 2 + j - half
                    out[shard, slot, head, j, slot, shard * heads_each + head, lane] = 1.0
    return out.reshape(shards * slots * heads_each * HD, slots * heads * LANES)


def local(
    activations,
    cotangent,
    lengths,
    positions,
    weights,
    first_moment,
    second_moment,
    vectors,
    vector_first,
    vector_second,
):
    tokens, width = activations.shape
    depth, slots, columns = weights.shape
    half = tokens // 2
    shards = lax.axis_size("zh")
    ys = lax.axis_size("y")
    xs = lax.axis_size("x")
    members = 2 * ys
    heads_each = columns // HD
    heads = shards * heads_each
    x, c, zh, zl, y = (lax.axis_index(a) for a in ("x", "c", "zh", "zl", "y"))
    me = zl * ys + y
    members_of = shards * members
    four = 4 * columns
    everyone = ("zh", "zl", "y", "x", "c")

    inputs = activations.astype(FULL)
    early_norm = layer_norm(inputs, vectors[0], vectors[1]).astype(LOW)

    low = weights.astype(LOW)
    lift = jnp.concatenate([low[:, 4:8, :].reshape(depth, four), low[:, 3, :]], axis=1)
    down = low[:, 8:12, :].reshape(depth, four)
    lift_all = lax.all_gather(lift, everyone, axis=0, tiled=True)
    lift_all = lift_all.reshape(members_of, width, four + columns)
    down_w = lax.all_gather(down, everyone, axis=0, tiled=True)
    down_w = down_w.reshape(members_of, width, four)
    lift_w = lift_all[:, :, :four]
    out_w = lift_all[:, :, four:]

    part = jnp.concatenate(gather(early_norm[:half], "y"), axis=0)
    rows_a = jnp.concatenate(gather(part, "zl"), axis=0)
    part = jnp.concatenate(gather(early_norm[half:], "zl"), axis=0).reshape(2, half, width)
    rows_b = jnp.stack(gather(part, "y"), axis=1).reshape(members * half, width)
    early_rows = jnp.concatenate([rows_a, rows_b], axis=0)

    qkv = low[:, 0:3, :].reshape(depth, 3 * columns)
    qkv = jnp.concatenate(settle(gather(qkv, "zh"), zh), axis=1)
    qkv = jnp.stack(settle(gather(qkv, "x"), x), axis=0)
    qkv = jnp.stack(settle(gather(qkv, "c"), c), axis=1).reshape(width, shards * 3 * columns)
    spread = spread_matrix(shards, 3, heads_each, True)
    spread_low = jnp.asarray(spread, LOW)
    wide_w = nn(qkv, spread_low).astype(LOW)
    shard_of = jnp.arange(shards) * members + me
    qkv_bias = jnp.take(vectors[6:9].reshape(3, -1, columns), shard_of, axis=1)
    qkv_bias = jnp.swapaxes(qkv_bias, 0, 1).reshape(1, -1)
    wide_bias = lax.dot(qkv_bias, jnp.asarray(spread), precision=lax.Precision.HIGHEST)

    counts = lax.dynamic_index_in_dim(lengths, zh, 0, keepdims=False)
    ends = jnp.cumsum(counts)
    spots = jnp.arange(SEQ, dtype=jnp.int32)
    ids = jnp.sum((spots[:, None] >= ends[None, :]).astype(jnp.int32), axis=1)
    blocks = 2 * members
    id_blocks = ids.reshape(blocks, half)
    low_spot = jnp.sum((ids[None, :] < id_blocks[:, :1]).astype(jnp.int32), axis=1)
    high_spot = jnp.sum((ids[None, :] <= id_blocks[:, -1:]).astype(jnp.int32), axis=1)
    info = jnp.concatenate(
        [me.reshape(1).astype(jnp.int32), low_spot // half, (high_spot + half - 1) // half]
    ).astype(jnp.int32)
    row_ids = ids.reshape(blocks, 1, half)
    column_ids = ids.reshape(SEQ, 1)

    spot = lax.dynamic_slice_in_dim(positions, zh * SEQ, SEQ, 1).reshape(2, members, 2, half)
    spot = jnp.take(spot, me ^ jnp.arange(members), axis=1)
    spot = jnp.swapaxes(spot, 1, 2).reshape(2, SEQ).astype(FULL)
    quarter = HD // 4
    freq = 10000.0 ** (-jnp.arange(quarter, dtype=FULL) * 4.0 / HD)
    angle = jnp.concatenate([spot[0][:, None] * freq, spot[1][:, None] * freq], axis=1)
    cosine, sine = jnp.cos(angle), jnp.sin(angle)
    gap = jnp.zeros((SEQ, LANES // 2 - HD // 2), FULL)
    cosine = jnp.concatenate([cosine, gap, cosine, gap], axis=1)
    sine = jnp.concatenate([-sine, gap, sine, gap], axis=1)

    query, keys, values, keys_t, values_t = project(
        info, early_rows, wide_w, wide_bias, cosine, sine, members, heads, []
    )
    pack = jnp.asarray(spread_matrix(1, 1, heads_each, False).T, LOW)
    spread_one = jnp.asarray(spread_matrix(1, 3, heads_each, True), LOW)
    own, logs, attended = [], [], []
    for group in range(shards):
        some, log = attend(
            info, query, keys, values_t, row_ids, column_ids, pack, heads_each, group, logs[-1:]
        )
        own.append(some)
        logs.append(log)
        some = some.reshape(members, tokens, columns)
        attended.append(lax.all_to_all(some, SQUARE, split_axis=0, concat_axis=0, tiled=True))

    attended = jnp.concatenate(attended, axis=0)
    branch = jnp.einsum("tnc,tic->ni", attended, out_w, preferred_element_type=FULL)
    middle = inputs + branch + vectors[4]
    later_norm = layer_norm(middle, vectors[2], vectors[3]).astype(LOW)

    lift_bias = jnp.swapaxes(vectors[9:13].reshape(4, members_of, columns), 0, 1)
    lift_bias = lift_bias.reshape(members_of, 1, four)
    upper = jnp.einsum("nd,tdj->tnj", later_norm, lift_w, preferred_element_type=FULL) + lift_bias
    hidden = quick_gelu(upper).astype(LOW)

    mixed = jnp.einsum("tnj,tij->ni", hidden, down_w, preferred_element_type=FULL)
    block_output = (middle + mixed + vectors[5]).astype(LOW)

    def split(value):
        value = value.reshape(tokens, xs, 2, depth)
        parts = [value[:, :, i].reshape(tokens, xs * depth) for i in range(2)]
        return jnp.where(c == 0, parts[0], parts[1]), jnp.where(c == 0, parts[1], parts[0])

    def first_sum(left, right):
        mine, theirs = left
        theirs = jnp.einsum("ni,tnj->tij", theirs, right, preferred_element_type=FULL)
        theirs = swap(theirs.astype(LOW), "c", 1).astype(FULL)
        mine = jnp.einsum("ni,tnj->tij", mine, right, preferred_element_type=FULL)
        return (mine + theirs).astype(LOW)

    step = depth // CHUNKS

    def chunk(value, k):
        value = value.reshape(2 * shards, ys, xs, CHUNKS, step, value.shape[-1])
        return value[:, :, :, k]

    def over_plane(value, order):
        first = scatter(value, order[0], 1 if order[0] == "y" else 2).astype(LOW)
        last = scatter(first, order[1], 1).astype(LOW)
        return first, last

    cot_parts = split(cotangent)
    down_sum = first_sum(cot_parts, hidden)
    down_plane = [over_plane(chunk(down_sum, 0), "yx"), over_plane(chunk(down_sum, 1), "xy")]
    down_grad = jnp.concatenate([scatter(last, LINE, 0) for _, last in down_plane], axis=0)

    hidden_grad = jnp.einsum("ni,tij->tnj", cotangent, down_w, preferred_element_type=FULL)
    upper_grad = jax.vjp(quick_gelu, upper)[1](hidden_grad)[0].astype(LOW)
    upper_grad = tie(upper_grad, down_sum)
    later_grad = jnp.einsum("tnj,tdj->nd", upper_grad, lift_w, preferred_element_type=FULL)

    cot_full = cotangent.astype(FULL)
    middle_part, gain_second, shift_second = jax.vjp(layer_norm, middle, vectors[2], vectors[3])[1](
        later_grad
    )
    middle_grad = cot_full + middle_part
    middle_low = middle_grad.astype(LOW)

    lift_sum = first_sum(split(later_norm), upper_grad)
    lift_plane = [over_plane(chunk(lift_sum, 0), "xy"), over_plane(chunk(lift_sum, 1), "yx")]
    lift_grad = jnp.concatenate([scatter(last, LINE, 0) for _, last in lift_plane], axis=0)

    attended_grad = jnp.einsum("ni,tic->tnc", middle_low, out_w, preferred_element_type=FULL)
    attended_grad = attended_grad.astype(LOW).reshape(shards, members, tokens, columns)
    row_grad = [
        lax.all_to_all(attended_grad[g], SQUARE, split_axis=0, concat_axis=0, tiled=True)
        for g in range(shards)
    ]
    out_grad = jnp.einsum("ni,tnc->tic", middle_low, attended, preferred_element_type=FULL)
    out_grad = out_grad.astype(LOW).reshape(members_of * width, columns)
    out_grad = lax.psum_scatter(out_grad, everyone, scatter_dimension=0, tiled=True).astype(FULL)

    heads_grad = []
    waits = [
        leaves([first for first, _ in down_plane]),
        leaves(([last for _, last in down_plane], [first for first, _ in lift_plane])),
    ]
    waits += [[]] * (shards - 2)
    for group in range(shards):
        heads_grad.append(
            attend_back(
                info,
                query,
                keys,
                values,
                keys_t,
                row_grad[group].reshape(SEQ, columns),
                own[group],
                logs[group],
                row_ids,
                column_ids,
                cosine,
                sine,
                pack,
                spread_one,
                members,
                heads_each,
                group,
                waits[group] + heads_grad[-1:],
            )
        )
    qkv = tie(qkv, heads_grad[-1], [last for _, last in lift_plane], down_grad)
    three = 3 * columns
    partial = sum(nt(some, qkv[:, g * three : (g + 1) * three]) for g, some in enumerate(heads_grad))
    partial = partial.astype(LOW).reshape(2, 2, ys, half, width)
    some = scatter_near([partial[0, l] for l in range(2)], "zl")
    some_a = scatter_near([some[j] for j in range(ys)], "y")
    some = scatter_near([partial[1, :, j] for j in range(ys)], "y")
    some_b = scatter_near([some[l] for l in range(2)], "zl")
    early_grad = jnp.concatenate([some_a, some_b], axis=0)

    qkv_grad = jnp.stack([tn(early_rows, some).astype(LOW) for some in heads_grad], axis=0)
    qkv_grad = qkv_grad.reshape(shards, xs, 2, depth, three)
    qkv_grad = scatter(qkv_grad, "c", 2).astype(LOW)
    qkv_grad = scatter(qkv_grad, "x", 1).astype(LOW)
    qkv_grad = scatter(qkv_grad, "zh", 0)

    input_part, gain_first, shift_first = jax.vjp(layer_norm, inputs, vectors[0], vectors[1])[1](
        early_grad
    )
    input_grad = (middle_grad + input_part).astype(LOW)

    owned = jnp.concatenate([qkv_grad, out_grad, lift_grad, down_grad], axis=1)
    owned = owned.reshape(depth, slots, columns)

    ffn_sum = jnp.sum(upper_grad, axis=1, dtype=FULL).reshape(members_of, 4, columns)
    ffn_bias = jnp.swapaxes(ffn_sum, 0, 1).reshape(4, width)
    ready = jnp.stack(
        [gain_second, shift_second, jnp.sum(middle_grad, axis=0), jnp.sum(cot_full, axis=0)]
    )
    heads_sum = jnp.stack([jnp.sum(some, axis=0, dtype=FULL) for some in heads_grad])
    heads_sum = heads_sum.reshape(shards, 3, columns)
    placed = jnp.where(
        (jnp.arange(members) == me)[None, None, :, None],
        jnp.swapaxes(heads_sum, 0, 1)[:, :, None, :],
        0.0,
    ).reshape(3, width)
    vector_grad = jnp.concatenate(
        [jnp.stack([gain_first, shift_first]), ready, placed, ffn_bias], axis=0
    )
    vector_grad = sum_everywhere(vector_grad)

    next_first, next_second, next_weights = adam_update(
        weights, owned, first_moment, second_moment, rate_matrix, decay_matrix
    )
    next_vector_first, next_vector_second, next_vectors = adam_update(
        vectors, vector_grad, vector_first, vector_second, rate_vector, 0.0
    )
    return (
        block_output,
        input_grad,
        next_first,
        next_second,
        next_weights,
        next_vector_first,
        next_vector_second,
        next_vectors,
    )


def solution(mesh):
    fsdp = mesh.shape["fsdp"]
    tp = mesh.shape["tp"]
    outer = ("x", "c")
    inner = ("zh", "zl", "y")

    def run(*args):
        rows = args[2].shape[0] // fsdp
        fine = Mesh(
            mesh.devices.reshape(fsdp // 2, 2, rows, 2, tp // (2 * rows)), outer + inner
        )
        patches = P(outer + inner, None)
        matrix = P(outer, None, inner)
        in_specs = (
            patches,
            patches,
            P(outer, None),
            P(None, outer),
            matrix,
            matrix,
            matrix,
            P(),
            P(),
            P(),
        )
        out_specs = (patches, patches, matrix, matrix, matrix, P(), P(), P())
        return jax.shard_map(
            local, mesh=fine, in_specs=in_specs, out_specs=out_specs, check_vma=False
        )(*args)

    return run
```

```python
import functools
import math

import jax
import jax.numpy as jnp
import numpy as np
from jax import lax
from jax.experimental import pallas as pl
from jax.experimental.pallas import tpu as pltpu
from jax.sharding import Mesh, PartitionSpec as P

HD = 80
LANES = 128
SEQ = 2048
STEP = 10
CHUNKS = 2

norm_eps = 1e-06
beta_first = 0.9
beta_second = 0.999
adam_eps = 1e-08
rate_matrix = 0.08
rate_vector = 0.6
decay_matrix = 0.05
gelu_slope = 1.702
masked_score = -1e30

LOW = jnp.bfloat16
FULL = jnp.float32
SQUARE = ("zl", "y")
LINE = ("zh", "zl")


def dot(a, b, dims):
    return lax.dot_general(a, b, (dims, ((), ())), preferred_element_type=FULL)


def nn(a, b):
    return dot(a, b, ((1,), (0,)))


def nt(a, b):
    return dot(a, b, ((1,), (1,)))


def tn(a, b):
    return dot(a, b, ((0,), (0,)))


def layer_norm(value, gain, shift):
    center = value - jnp.mean(value, axis=-1, keepdims=True)
    spread = jnp.mean(center * center, axis=-1, keepdims=True)
    return center * lax.rsqrt(spread + norm_eps) * gain + shift


def quick_gelu(value):
    return value * jax.nn.sigmoid(gelu_slope * value)


def adam_update(param, grad, first, second, rate, decay):
    first = beta_first * first + (1.0 - beta_first) * grad
    second = beta_second * second + (1.0 - beta_second) * grad * grad
    first_hat = first / (1.0 - beta_first**STEP)
    second_hat = second / (1.0 - beta_second**STEP)
    fresh = param - rate * (first_hat / (jnp.sqrt(second_hat) + adam_eps) + decay * param)
    return (first, second, fresh)


def swap(value, axis, far):
    return lax.ppermute(value, axis, [(i, i ^ far) for i in range(lax.axis_size(axis))])


def gather(value, axis):
    return [value] + [swap(value, axis, far) for far in range(1, lax.axis_size(axis))]


def settle(pieces, spot):
    bit = 1
    while bit < len(pieces):
        turned = (spot // bit) % 2 == 1
        pieces = [jnp.where(turned, pieces[i ^ bit], pieces[i]) for i in range(len(pieces))]
        bit *= 2
    return pieces


def scatter(value, axis, dim):
    spot = lax.axis_index(axis)

    def part(far):
        return lax.dynamic_index_in_dim(value, spot ^ far, dim, keepdims=False)

    total = part(0).astype(FULL)
    for far in range(1, lax.axis_size(axis)):
        total = total + swap(part(far).astype(LOW), axis, far).astype(FULL)
    return total


def scatter_near(pieces, axis):
    total = pieces[0].astype(FULL)
    for far in range(1, len(pieces)):
        total = total + swap(pieces[far].astype(LOW), axis, far).astype(FULL)
    return total


def leaves(things):
    return jax.tree.leaves(things)


def tie(value, *earlier):
    first = leaves(earlier)
    return pl.pallas_call(
        lambda *refs: None,
        in_specs=[pl.BlockSpec(memory_space=pl.ANY)] * (1 + len(first)),
        out_specs=pl.BlockSpec(memory_space=pl.ANY),
        out_shape=jax.ShapeDtypeStruct(value.shape, value.dtype),
        input_output_aliases={0: 0},
        name="tie",
    )(value, *first)


def sum_everywhere(value):
    for axis, size in (("c", 2), (("x", "y"), lax.axis_size("x") * lax.axis_size("y")), (LINE, 2 * lax.axis_size("zh"))):
        far = 1
        while far < size:
            if far * 4 <= size:
                one, two, three = (swap(value, axis, k * far) for k in (1, 2, 3))
                value = (value + one) + (two + three)
                far *= 4
            else:
                value = value + swap(value, axis, far)
                far *= 2
    return value


def project_kernel(heads, info_ref, rows_ref, w_ref, bias_ref, cos_ref, sin_ref, *refs):
    q_ref, k_ref, v_ref, kt_ref, vt_ref = refs[-5:]
    wide = heads * LANES
    cosine = cos_ref[...]
    sine = sin_ref[...]
    rows = rows_ref[...]
    factor = HD ** (-0.5) * math.log2(math.e)
    for slot in range(3):
        out = nn(rows, w_ref[:, slot * wide : (slot + 1) * wide])
        out = out + bias_ref[:, slot * wide : (slot + 1) * wide]
        for head in range(heads):
            lanes = slice(head * LANES, (head + 1) * LANES)
            value = out[:, lanes]
            if slot < 2:
                value = value * cosine + pltpu.roll(value, LANES // 2, 1) * sine
            if slot == 0:
                q_ref[:, lanes] = (value * factor).astype(LOW)
            elif slot == 1:
                k_ref[:, lanes] = value.astype(LOW)
                kt_ref[lanes, :] = value.T.astype(LOW)
            else:
                v_ref[:, lanes] = value.astype(LOW)
                vt_ref[lanes, :] = value.T.astype(LOW)


def project(info, rows, wide_w, wide_bias, cosine, sine, members, heads, earlier):
    total, width = rows.shape
    tile = total // (2 * members)
    wide = heads * LANES

    def place(g, info):
        return ((g % members) ^ info[0]) * 2 + g // members

    flat = pl.BlockSpec((tile, wide), lambda g, info: (place(g, info), 0))
    tall = pl.BlockSpec((wide, tile), lambda g, info: (0, place(g, info)))
    return pl.pallas_call(
        functools.partial(project_kernel, heads),
        grid_spec=pltpu.PrefetchScalarGridSpec(
            num_scalar_prefetch=1,
            grid=(2 * members,),
            in_specs=[
                pl.BlockSpec((tile, width), lambda g, info: (g, 0)),
                pl.BlockSpec((width, 3 * wide), lambda g, info: (0, 0)),
                pl.BlockSpec((1, 3 * wide), lambda g, info: (0, 0)),
                pl.BlockSpec((tile, LANES), lambda g, info: (g, 0)),
                pl.BlockSpec((tile, LANES), lambda g, info: (g, 0)),
            ]
            + [pl.BlockSpec(memory_space=pl.ANY)] * len(earlier),
            out_specs=[flat, flat, flat, tall, tall],
        ),
        out_shape=[jax.ShapeDtypeStruct((total, wide), LOW)] * 3
        + [jax.ShapeDtypeStruct((wide, total), LOW)] * 2,
        compiler_params=pltpu.CompilerParams(vmem_limit_bytes=48 << 20),
        cost_estimate=pl.CostEstimate(
            flops=2 * total * width * 3 * wide,
            bytes_accessed=2 * total * (width + 5 * wide) + 6 * width * wide,
            transcendentals=0,
        ),
        name="project",
    )(info, rows, wide_w, wide_bias, cosine, sine, *earlier)


def attend_kernel(heads, tile, info_ref, q_ref, k_ref, vt_ref, row_ids, column_ids, pack_ref, *refs):
    out_ref, lse_ref, acc_ref = refs[-3:]
    block = pl.program_id(0)
    first = info_ref[1 + block]
    last = info_ref[1 + pl.num_programs(0) + block]
    acc_ref[...] = jnp.zeros_like(acc_ref)
    mine = row_ids[0]

    def step(index, carry):
        start = pl.multiple_of(index * tile, tile)
        theirs = column_ids[pl.ds(start, tile), :]
        allowed = theirs == mine
        fresh = []
        for head in range(heads):
            lanes = slice(head * LANES, (head + 1) * LANES)
            top, summed = carry[head]
            scores = nt(k_ref[pl.ds(start, tile), lanes], q_ref[:, lanes])
            scores = jnp.where(allowed, scores, masked_score)
            higher = jnp.maximum(top, jnp.max(scores, axis=0, keepdims=True))
            shrink = jnp.exp2(top - higher)
            expo = jnp.exp2(scores - higher)
            summed = summed * shrink + jnp.sum(expo, axis=0, keepdims=True)
            part = nn(vt_ref[lanes, pl.ds(start, tile)], expo.astype(LOW))
            acc_ref[lanes, :] = acc_ref[lanes, :] * shrink + part
            fresh.append((higher, summed))
        return tuple(fresh)

    blank = (jnp.full((1, tile), masked_score, FULL), jnp.zeros((1, tile), FULL))
    done = lax.fori_loop(first, last, step, (blank,) * heads)
    for head in range(heads):
        lanes = slice(head * LANES, (head + 1) * LANES)
        top, summed = done[head]
        acc_ref[lanes, :] = acc_ref[lanes, :] / summed
        lse_ref[0, head : head + 1, :] = top + jnp.log2(summed)
    out_ref[...] = tn(acc_ref[...].astype(LOW), pack_ref[...]).astype(LOW)


def attend(info, query, keys, values_t, row_ids, column_ids, pack, heads, group, earlier):
    total = query.shape[0]
    wide = heads * LANES
    blocks, _, tile = row_ids.shape

    return pl.pallas_call(
        functools.partial(attend_kernel, heads, tile),
        grid_spec=pltpu.PrefetchScalarGridSpec(
            num_scalar_prefetch=1,
            grid=(blocks,),
            in_specs=[
                pl.BlockSpec((tile, wide), lambda b, info: (b, group)),
                pl.BlockSpec((total, wide), lambda b, info: (0, group)),
                pl.BlockSpec((wide, total), lambda b, info: (group, 0)),
                pl.BlockSpec((1, 1, tile), lambda b, info: (b, 0, 0)),
                pl.BlockSpec((total, 1), lambda b, info: (0, 0)),
                pl.BlockSpec(pack.shape, lambda b, info: (0, 0)),
            ]
            + [pl.BlockSpec(memory_space=pl.ANY)] * len(earlier),
            out_specs=[
                pl.BlockSpec((tile, heads * HD), lambda b, info: (b, 0)),
                pl.BlockSpec((1, heads, tile), lambda b, info: (b, 0, 0)),
            ],
            scratch_shapes=[pltpu.VMEM((wide, tile), FULL)],
        ),
        out_shape=[
            jax.ShapeDtypeStruct((total, heads * HD), LOW),
            jax.ShapeDtypeStruct((blocks, heads, tile), FULL),
        ],
        compiler_params=pltpu.CompilerParams(vmem_limit_bytes=48 << 20),
        cost_estimate=pl.CostEstimate(
            flops=2 * total * total * wide, bytes_accessed=8 * total * wide, transcendentals=total * total * heads // 2
        ),
        name="attend",
    )(info, query, keys, values_t, row_ids, column_ids, pack, *earlier)


def attend_back_kernel(
    heads,
    tile,
    members,
    info_ref,
    q_ref,
    k_ref,
    v_ref,
    kt_ref,
    grad_ref,
    o_ref,
    lse_ref,
    row_ids,
    column_ids,
    cos_ref,
    sin_ref,
    pack_ref,
    spread_ref,
    *refs,
):
    out_ref, inner_ref, do_ref, qt_ref, dk_ref, dv_ref = refs[-6:]
    block = pl.program_id(0)
    blocks = pl.num_programs(0)
    me = info_ref[0]
    first = info_ref[1 + block]
    last = info_ref[1 + blocks + block]
    wide = heads * LANES

    def place(b):
        return pl.multiple_of(b * tile, tile)

    def home(b):
        return pl.multiple_of(((b % 2) * members + ((b // 2) ^ me)) * tile, tile)

    def unrotate(value, b):
        where = pl.ds(home(b), tile)
        return value * cos_ref[where, :] - pltpu.roll(value, LANES // 2, 1) * sin_ref[where, :]

    @pl.when(block == 0)
    def _():
        qt_ref[...] = jnp.zeros_like(qt_ref)

        lane = lax.broadcasted_iota(jnp.int32, (8, heads * HD), 1)
        head = lax.broadcasted_iota(jnp.int32, (8, heads * HD), 0)
        pick = ((lane >= head * HD) & (lane < (head + 1) * HD)).astype(FULL)

        def fill(b, carry):
            where = pl.ds(place(b), tile)
            grad = grad_ref[where, :]
            do_ref[where, :] = nt(grad, pack_ref[...]).astype(LOW)
            both = o_ref[where, :].astype(FULL) * grad.astype(FULL)
            inner_ref[b] = lax.dot_general(
                pick,
                both,
                (((1,), (1,)), ((), ())),
                precision=lax.Precision.HIGHEST,
                preferred_element_type=FULL,
            )
            return carry

        lax.fori_loop(0, blocks, fill, 0)

    dk_ref[...] = jnp.zeros_like(dk_ref)
    dv_ref[...] = jnp.zeros_like(dv_ref)
    here = pl.ds(place(block), tile)
    theirs = column_ids[pl.ds(pl.multiple_of(block * tile, tile), tile), :]

    def step(index, carry):
        where = pl.ds(place(index), tile)
        allowed = theirs == row_ids[index]
        for head in range(heads):
            lanes = slice(head * LANES, (head + 1) * LANES)
            query = q_ref[where, lanes]
            grad = do_ref[where, lanes]
            scores = nt(k_ref[here, lanes], query)
            scores = jnp.where(allowed, scores, masked_score)
            probs = jnp.exp2(scores - lse_ref[index, head : head + 1, :])
            prob_grad = nt(v_ref[here, lanes], grad)
            score_grad = (probs * (prob_grad - inner_ref[index, head : head + 1, :])).astype(LOW)
            dv_ref[:, lanes] += nn(probs.astype(LOW), grad)
            dk_ref[:, lanes] += nn(score_grad, query)
            qt_ref[lanes, where] += nn(kt_ref[lanes, here], score_grad)
        return carry

    lax.fori_loop(first, last, step, 0)
    rows = pl.ds(home(block), tile)
    for head in range(heads):
        lanes = slice(head * LANES, (head + 1) * LANES)
        dk_ref[:, lanes] = unrotate(dk_ref[:, lanes] * math.log(2.0), block)
    key_part = nt(dk_ref[...].astype(LOW), spread_ref[:, wide : 2 * wide])
    value_part = nt(dv_ref[...].astype(LOW), spread_ref[:, 2 * wide :])
    out_ref[rows, :] = (key_part + value_part).astype(LOW)

    @pl.when(block == blocks - 1)
    def _():
        def spill(b, carry):
            rows = pl.ds(home(b), tile)
            for head in range(heads):
                lanes = slice(head * LANES, (head + 1) * LANES)
                query_grad = qt_ref[lanes, pl.ds(place(b), tile)].T * HD ** (-0.5)
                dk_ref[:, lanes] = unrotate(query_grad, b)
            query_part = nt(dk_ref[...].astype(LOW), spread_ref[:, :wide])
            out_ref[rows, :] = (out_ref[rows, :].astype(FULL) + query_part).astype(LOW)
            return carry

        lax.fori_loop(0, blocks, spill, 0)


def attend_back(info, query, keys, values, keys_t, grad, attended, logs, row_ids, column_ids, cosine, sine, pack, spread, members, heads, group, earlier):
    total = query.shape[0]
    wide = heads * LANES
    blocks, _, tile = row_ids.shape

    def whole(*shape):
        return pl.BlockSpec(shape, lambda b, info: (0,) * len(shape), pipeline_mode=pl.Buffered(1))

    flat = pl.BlockSpec((total, wide), lambda b, info: (0, group), pipeline_mode=pl.Buffered(1))
    tall = pl.BlockSpec((wide, total), lambda b, info: (group, 0), pipeline_mode=pl.Buffered(1))

    return pl.pallas_call(
        functools.partial(attend_back_kernel, heads, tile, members),
        grid_spec=pltpu.PrefetchScalarGridSpec(
            num_scalar_prefetch=1,
            grid=(blocks,),
            in_specs=[
                flat,
                flat,
                flat,
                tall,
                whole(total, heads * HD),
                whole(total, heads * HD),
                whole(blocks, heads, tile),
                whole(blocks, 1, tile),
                whole(total, 1),
                whole(total, LANES),
                whole(total, LANES),
                whole(*pack.shape),
                whole(*spread.shape),
            ]
            + [pl.BlockSpec(memory_space=pl.ANY)] * len(earlier),
            out_specs=whole(total, 3 * heads * HD),
            scratch_shapes=[
                pltpu.VMEM((blocks, 8, tile), FULL),
                pltpu.VMEM((total, wide), LOW),
                pltpu.VMEM((wide, total), FULL),
                pltpu.VMEM((tile, wide), FULL),
                pltpu.VMEM((tile, wide), FULL),
            ],
        ),
        out_shape=jax.ShapeDtypeStruct((total, 3 * heads * HD), LOW),
        compiler_params=pltpu.CompilerParams(vmem_limit_bytes=56 << 20),
        cost_estimate=pl.CostEstimate(
            flops=5 * total * total * wide, bytes_accessed=18 * total * wide, transcendentals=total * total * heads // 2
        ),
        name="attend_back",
    )(
        info,
        query,
        keys,
        values,
        keys_t,
        grad,
        attended,
        logs,
        row_ids,
        column_ids,
        cosine,
        sine,
        pack,
        spread,
        *earlier,
    )


def spread_matrix(shards, slots, heads_each, turned):
    heads = shards * heads_each
    out = np.zeros((shards, slots, heads_each, HD, slots, heads, LANES), np.float32)
    half = HD // 2
    for shard in range(shards):
        for slot in range(slots):
            for head in range(heads_each):
                for j in range(HD):
                    lane = j
                    if turned and slot < 2 and j >= half:
                        lane = LANES // 2 + j - half
                    out[shard, slot, head, j, slot, shard * heads_each + head, lane] = 1.0
    return out.reshape(shards * slots * heads_each * HD, slots * heads * LANES)


def local(
    activations,
    cotangent,
    lengths,
    positions,
    weights,
    first_moment,
    second_moment,
    vectors,
    vector_first,
    vector_second,
):
    tokens, width = activations.shape
    depth, slots, columns = weights.shape
    half = tokens // 2
    shards = lax.axis_size("zh")
    ys = lax.axis_size("y")
    xs = lax.axis_size("x")
    members = 2 * ys
    heads_each = columns // HD
    heads = shards * heads_each
    x, c, zh, zl, y = (lax.axis_index(a) for a in ("x", "c", "zh", "zl", "y"))
    me = zl * ys + y
    members_of = shards * members
    four = 4 * columns
    everyone = ("zh", "zl", "y", "x", "c")

    inputs = activations.astype(FULL)
    early_norm = layer_norm(inputs, vectors[0], vectors[1]).astype(LOW)

    low = weights.astype(LOW)
    lift = jnp.concatenate([low[:, 4:8, :].reshape(depth, four), low[:, 3, :]], axis=1)
    down = low[:, 8:12, :].reshape(depth, four)
    lift_all = lax.all_gather(lift, everyone, axis=0, tiled=True)
    lift_all = lift_all.reshape(members_of, width, four + columns)
    down_w = lax.all_gather(down, everyone, axis=0, tiled=True)
    down_w = down_w.reshape(members_of, width, four)
    lift_w = lift_all[:, :, :four]
    out_w = lift_all[:, :, four:]

    part = jnp.concatenate(gather(early_norm[:half], "y"), axis=0)
    rows_a = jnp.concatenate(gather(part, "zl"), axis=0)
    part = jnp.concatenate(gather(early_norm[half:], "zl"), axis=0).reshape(2, half, width)
    rows_b = jnp.stack(gather(part, "y"), axis=1).reshape(members * half, width)
    early_rows = jnp.concatenate([rows_a, rows_b], axis=0)

    qkv = low[:, 0:3, :].reshape(depth, 3 * columns)
    qkv = jnp.concatenate(settle(gather(qkv, "zh"), zh), axis=1)
    qkv = jnp.stack(settle(gather(qkv, "x"), x), axis=0)
    qkv = jnp.stack(settle(gather(qkv, "c"), c), axis=1).reshape(width, shards * 3 * columns)
    spread = spread_matrix(shards, 3, heads_each, True)
    spread_low = jnp.asarray(spread, LOW)
    wide_w = nn(qkv, spread_low).astype(LOW)
    shard_of = jnp.arange(shards) * members + me
    qkv_bias = jnp.take(vectors[6:9].reshape(3, -1, columns), shard_of, axis=1)
    qkv_bias = jnp.swapaxes(qkv_bias, 0, 1).reshape(1, -1)
    wide_bias = lax.dot(qkv_bias, jnp.asarray(spread), precision=lax.Precision.HIGHEST)

    counts = lax.dynamic_index_in_dim(lengths, zh, 0, keepdims=False)
    ends = jnp.cumsum(counts)
    spots = jnp.arange(SEQ, dtype=jnp.int32)
    ids = jnp.sum((spots[:, None] >= ends[None, :]).astype(jnp.int32), axis=1)
    blocks = 2 * members
    id_blocks = ids.reshape(blocks, half)
    low_spot = jnp.sum((ids[None, :] < id_blocks[:, :1]).astype(jnp.int32), axis=1)
    high_spot = jnp.sum((ids[None, :] <= id_blocks[:, -1:]).astype(jnp.int32), axis=1)
    info = jnp.concatenate(
        [me.reshape(1).astype(jnp.int32), low_spot // half, (high_spot + half - 1) // half]
    ).astype(jnp.int32)
    row_ids = ids.reshape(blocks, 1, half)
    column_ids = ids.reshape(SEQ, 1)

    spot = lax.dynamic_slice_in_dim(positions, zh * SEQ, SEQ, 1).reshape(2, members, 2, half)
    spot = jnp.take(spot, me ^ jnp.arange(members), axis=1)
    spot = jnp.swapaxes(spot, 1, 2).reshape(2, SEQ).astype(FULL)
    quarter = HD // 4
    freq = 10000.0 ** (-jnp.arange(quarter, dtype=FULL) * 4.0 / HD)
    angle = jnp.concatenate([spot[0][:, None] * freq, spot[1][:, None] * freq], axis=1)
    cosine, sine = jnp.cos(angle), jnp.sin(angle)
    gap = jnp.zeros((SEQ, LANES // 2 - HD // 2), FULL)
    cosine = jnp.concatenate([cosine, gap, cosine, gap], axis=1)
    sine = jnp.concatenate([-sine, gap, sine, gap], axis=1)

    query, keys, values, keys_t, values_t = project(
        info, early_rows, wide_w, wide_bias, cosine, sine, members, heads, []
    )
    pack = jnp.asarray(spread_matrix(1, 1, heads_each, False).T, LOW)
    spread_one = jnp.asarray(spread_matrix(1, 3, heads_each, True), LOW)
    own, logs, attended = [], [], []
    for group in range(shards):
        some, log = attend(
            info, query, keys, values_t, row_ids, column_ids, pack, heads_each, group, logs[-1:]
        )
        own.append(some)
        logs.append(log)
        some = some.reshape(members, tokens, columns)
        attended.append(lax.all_to_all(some, SQUARE, split_axis=0, concat_axis=0, tiled=True))

    attended = jnp.concatenate(attended, axis=0)
    branch = jnp.einsum("tnc,tic->ni", attended, out_w, preferred_element_type=FULL)
    middle = inputs + branch + vectors[4]
    later_norm = layer_norm(middle, vectors[2], vectors[3]).astype(LOW)

    lift_bias = jnp.swapaxes(vectors[9:13].reshape(4, members_of, columns), 0, 1)
    lift_bias = lift_bias.reshape(members_of, 1, four)
    upper = jnp.einsum("nd,tdj->tnj", later_norm, lift_w, preferred_element_type=FULL) + lift_bias
    hidden = quick_gelu(upper).astype(LOW)

    mixed = jnp.einsum("tnj,tij->ni", hidden, down_w, preferred_element_type=FULL)
    block_output = (middle + mixed + vectors[5]).astype(LOW)

    def split(value):
        value = value.reshape(tokens, xs, 2, depth)
        parts = [value[:, :, i].reshape(tokens, xs * depth) for i in range(2)]
        return jnp.where(c == 0, parts[0], parts[1]), jnp.where(c == 0, parts[1], parts[0])

    def first_sum(left, right):
        mine, theirs = left
        theirs = jnp.einsum("ni,tnj->tij", theirs, right, preferred_element_type=FULL)
        theirs = swap(theirs.astype(LOW), "c", 1).astype(FULL)
        mine = jnp.einsum("ni,tnj->tij", mine, right, preferred_element_type=FULL)
        return (mine + theirs).astype(LOW)

    step = depth // CHUNKS

    def chunk(value, k):
        value = value.reshape(2 * shards, ys, xs, CHUNKS, step, value.shape[-1])
        return value[:, :, :, k]

    def over_plane(value, order):
        first = scatter(value, order[0], 1 if order[0] == "y" else 2).astype(LOW)
        last = scatter(first, order[1], 1).astype(LOW)
        return first, last

    cot_parts = split(cotangent)
    down_sum = first_sum(cot_parts, hidden)
    down_plane = [over_plane(chunk(down_sum, 0), "yx"), over_plane(chunk(down_sum, 1), "xy")]
    down_grad = jnp.concatenate([scatter(last, LINE, 0) for _, last in down_plane], axis=0)

    hidden_grad = jnp.einsum("ni,tij->tnj", cotangent, down_w, preferred_element_type=FULL)
    upper_grad = jax.vjp(quick_gelu, upper)[1](hidden_grad)[0].astype(LOW)
    upper_grad = tie(upper_grad, down_sum)
    later_grad = jnp.einsum("tnj,tdj->nd", upper_grad, lift_w, preferred_element_type=FULL)

    cot_full = cotangent.astype(FULL)
    middle_part, gain_second, shift_second = jax.vjp(layer_norm, middle, vectors[2], vectors[3])[1](
        later_grad
    )
    middle_grad = cot_full + middle_part
    middle_low = middle_grad.astype(LOW)

    lift_sum = first_sum(split(later_norm), upper_grad)
    lift_plane = [over_plane(chunk(lift_sum, 0), "xy"), over_plane(chunk(lift_sum, 1), "yx")]
    lift_grad = jnp.concatenate([scatter(last, LINE, 0) for _, last in lift_plane], axis=0)

    attended_grad = jnp.einsum("ni,tic->tnc", middle_low, out_w, preferred_element_type=FULL)
    attended_grad = attended_grad.astype(LOW).reshape(shards, members, tokens, columns)
    row_grad = [
        lax.all_to_all(attended_grad[g], SQUARE, split_axis=0, concat_axis=0, tiled=True)
        for g in range(shards)
    ]
    out_grad = jnp.einsum("ni,tnc->tic", middle_low, attended, preferred_element_type=FULL)
    out_grad = out_grad.astype(LOW).reshape(members_of * width, columns)
    out_grad = lax.psum_scatter(out_grad, everyone, scatter_dimension=0, tiled=True).astype(FULL)

    heads_grad = []
    waits = [
        leaves([first for first, _ in down_plane]),
        leaves(([last for _, last in down_plane], [first for first, _ in lift_plane])),
    ]
    waits += [[]] * (shards - 2)
    for group in range(shards):
        heads_grad.append(
            attend_back(
                info,
                query,
                keys,
                values,
                keys_t,
                row_grad[group].reshape(SEQ, columns),
                own[group],
                logs[group],
                row_ids,
                column_ids,
                cosine,
                sine,
                pack,
                spread_one,
                members,
                heads_each,
                group,
                waits[group] + heads_grad[-1:],
            )
        )
    qkv = tie(qkv, heads_grad[-1], [last for _, last in lift_plane], down_grad)
    three = 3 * columns
    partial = sum(nt(some, qkv[:, g * three : (g + 1) * three]) for g, some in enumerate(heads_grad))
    partial = partial.astype(LOW).reshape(2, 2, ys, half, width)
    heads_grad[-1] = tie(heads_grad[-1], partial)
    some = scatter_near([partial[0, l] for l in range(2)], "zl")
    some_a = scatter_near([some[j] for j in range(ys)], "y")
    some = scatter_near([partial[1, :, j] for j in range(ys)], "y")
    some_b = scatter_near([some[l] for l in range(2)], "zl")
    early_grad = jnp.concatenate([some_a, some_b], axis=0)

    qkv_grad = jnp.stack([tn(early_rows, some).astype(LOW) for some in heads_grad], axis=0)
    qkv_grad = qkv_grad.reshape(shards, xs, 2, depth, three)
    qkv_grad = scatter(qkv_grad, "c", 2).astype(LOW)
    qkv_grad = scatter(qkv_grad, "x", 1).astype(LOW)
    qkv_grad = scatter(qkv_grad, "zh", 0)

    input_part, gain_first, shift_first = jax.vjp(layer_norm, inputs, vectors[0], vectors[1])[1](
        early_grad
    )
    input_grad = (middle_grad + input_part).astype(LOW)

    owned = jnp.concatenate([qkv_grad, out_grad, lift_grad, down_grad], axis=1)
    owned = owned.reshape(depth, slots, columns)

    ffn_sum = jnp.sum(upper_grad, axis=1, dtype=FULL).reshape(members_of, 4, columns)
    ffn_bias = jnp.swapaxes(ffn_sum, 0, 1).reshape(4, width)
    ready = jnp.stack(
        [gain_second, shift_second, jnp.sum(middle_grad, axis=0), jnp.sum(cot_full, axis=0)]
    )
    heads_sum = jnp.stack([jnp.sum(some, axis=0, dtype=FULL) for some in heads_grad])
    heads_sum = heads_sum.reshape(shards, 3, columns)
    placed = jnp.where(
        (jnp.arange(members) == me)[None, None, :, None],
        jnp.swapaxes(heads_sum, 0, 1)[:, :, None, :],
        0.0,
    ).reshape(3, width)
    vector_grad = jnp.concatenate(
        [jnp.stack([gain_first, shift_first]), ready, placed, ffn_bias], axis=0
    )
    vector_grad = sum_everywhere(vector_grad)

    next_first, next_second, next_weights = adam_update(
        weights, owned, first_moment, second_moment, rate_matrix, decay_matrix
    )
    next_vector_first, next_vector_second, next_vectors = adam_update(
        vectors, vector_grad, vector_first, vector_second, rate_vector, 0.0
    )
    return (
        block_output,
        input_grad,
        next_first,
        next_second,
        next_weights,
        next_vector_first,
        next_vector_second,
        next_vectors,
    )


def solution(mesh):
    fsdp = mesh.shape["fsdp"]
    tp = mesh.shape["tp"]
    outer = ("x", "c")
    inner = ("zh", "zl", "y")

    def run(*args):
        rows = args[2].shape[0] // fsdp
        fine = Mesh(
            mesh.devices.reshape(fsdp // 2, 2, rows, 2, tp // (2 * rows)), outer + inner
        )
        patches = P(outer + inner, None)
        matrix = P(outer, None, inner)
        in_specs = (
            patches,
            patches,
            P(outer, None),
            P(None, outer),
            matrix,
            matrix,
            matrix,
            P(),
            P(),
            P(),
        )
        out_specs = (patches, patches, matrix, matrix, matrix, P(), P(), P())
        return jax.shard_map(
            local, mesh=fine, in_specs=in_specs, out_specs=out_specs, check_vma=False
        )(*args)

    return run
```
